128 devices in a mesh: hg: 4 (over x), grp: 8 (over y, core), side: 4 (over z).
Axes of the slice: x: 4, y: 4, z: 4, core: 2. Of those that a mesh axis runs over, the one named last changes fastest.
Arguments:
- q_nope: bfloat16 [128, 8192], P(('grp', 'side'), 'hg'), may hold values from -6 to 6
- q_rope: bfloat16 [128, 4096], P(('grp', 'side'), 'hg'), may hold values from -16 to 16
- w_absorb: bfloat16 [64, 128, 512], P('hg'), may hold values from -0.5 to 0.5
- cache_latent: bfloat16 [64, 4096, 512], P(('grp', 'side')), may hold values from -6 to 6
- cache_rope: bfloat16 [64, 64, 4096], P(('grp', 'side')), may hold values from -512 to 512
- lengths: int32 [64], P(('grp', 'side')), may hold values from 4 to 4096, as said below
- w_value: bfloat16 [64, 512, 128], P('hg'), may hold values from -2 to 2
- w_out: bfloat16 [8192, 7168], P('hg', ('grp', 'side')), may hold values from -0.0625 to 0.0625
- residual: bfloat16 [128, 7168], P(('grp', 'side')), may hold values from -6 to 6
- norm_gain: bfloat16 [7168], replicated, may hold values from 0.5 to 1.5
- routes: int32 [128, 4], P(('grp', 'side')), may hold values from 0 to 15, all different within a row; in each aligned block of 4 rows (0 to 3, 4 to 7, ...) at most 2 rows name the same one
- gate_int: int32 [128, 4], P(('grp', 'side')), may hold values from 1 to 255
- w_gate: bfloat16 [16, 7168, 2048], P('grp', None, ('hg', 'side')), may hold values from -0.0625 to 0.0625
- w_up: bfloat16 [16, 7168, 2048], P('grp', None, ('hg', 'side')), may hold values from -0.0625 to 0.0625
- w_down: bfloat16 [16, 2048, 7168], P('grp', ('hg', 'side')), may hold values from -0.125 to 0.125
Outputs:
- layer_out: bfloat16 [128, 7168], P(('grp', 'side'), 'hg')
The draws below stay inside these ranges and needn't reach their ends.
Inputs may be any that keep to these rules, and one draw needn't show every extreme that they name: `lengths`: one request in every draw has exactly 4096 filled positions. `routes`: each row names 4 different experts; among the 4 tokens of one index of grp and side, no expert is named by more than 2 tokens, a bound that some block reaches.
All inputs are finite; a program needn't handle non-finite values.
Results may differ from the reference program's by a relative error of at most 0.0095.
Values may be sent and summed in bfloat16 or wider, within the bound.
No kernel may reach another device: no remote copies, remote signals or barrier semaphores. Data moves between devices by JAX's collectives and lax.ppermute only.
A program may use at most 192 MiB of HBM per device.

```python
import math
import jax
import jax.numpy as jnp
import numpy as np
from jax import lax

D = 7168
LAT = 512
ROPE = 64
NOPE = 128
VDIM = 128
FFE = 2048
QPR = 2
LEN = 4096
TOPK = 4
HEADS = 64
TOK_DEV = 4
REQS = 64
TOKENS = 128
EXPERTS = 16
CAP = 2
N_GRP = 8
N_SIDE = 4


def draw_q_rope(key, part):
    key = jax.random.fold_in(key, 11)
    noise = jnp.clip(jax.random.normal(key, (TOKENS, HEADS, ROPE), jnp.float32), -6.0, 6.0)
    values = noise
    return values.reshape(TOKENS, HEADS * ROPE).astype(jnp.bfloat16)


def draw_cache_rope(key, part):
    key = jax.random.fold_in(key, 12)
    values = jnp.clip(jax.random.normal(key, (REQS, ROPE, LEN), jnp.float32), -6.0, 6.0)
    return values.astype(jnp.bfloat16)


def draw_lengths(key, part):
    key = jax.random.fold_in(key, 13)
    first, second = jax.random.split(key)
    values = jax.random.randint(first, (REQS,), QPR + 2, LEN + 1)
    pick = jax.random.randint(second, (), 0, REQS)
    return jnp.where(jnp.arange(REQS) == pick, LEN, values).astype(jnp.int32)


def plant(values, own_key, low, largest):
    index_at = [jax.random.randint(jax.random.fold_in(own_key, axis), (), 0, length) for axis, length in enumerate(values.shape)]
    longest = values.shape.index(max(values.shape))
    beside = index_at[:longest] + [(index_at[longest] + 1) % values.shape[longest]] + index_at[longest + 1:]
    return values.at[tuple(index_at)].set(low).at[tuple(beside)].set(largest)


def shard_levels(rng, shape, pieces, least, top_value):
    def one(dim, shards_of):
        draws = jax.random.uniform(jax.random.fold_in(jax.random.fold_in(rng, 6), dim), (shards_of,), jnp.float32, least / len(pieces), top_value / len(pieces))
        return jnp.repeat(jnp.exp(draws), shape[dim] // shards_of).reshape((-1,) + (1,) * (len(shape) - dim - 1))

    level = one(*pieces[0])
    for cut in pieces[1:]:
        level = level * one(*cut)
    return level


def assign_block(stream_key, own, number, rows, amount, top, most, skew):
    sequence = jax.random.permutation(stream_key, amount)
    crowded, common = shares(amount, rows * top, most, skew, True), shares(amount, rows * top, most, skew, False)
    places = jnp.arange(amount)

    def named(sizes, turn):
        used = int((sizes > 0).sum())
        fixed = max(1, used // 4)
        passed = fixed + (places - fixed + turn * (used - fixed)) % max(1, amount - fixed)
        return jnp.zeros((amount,), jnp.int32).at[sequence[jnp.where(places < fixed, places, passed)]].set(jnp.asarray(sizes, jnp.int32))

    sizes = jnp.where(number % 4 == 0, named(crowded, number // 4), named(common, number - number // 4 - 1))
    mixed = jax.random.permutation(jax.random.fold_in(own, 3), amount)
    giver, taker = mixed[0:amount // 2 * 2:2], mixed[1:amount // 2 * 2:2]
    slack = jnp.minimum(sizes[giver] - 1, most - sizes[taker]) // 2
    slack = jnp.where((giver == sequence[0]) | (taker == sequence[0]) | (sizes[taker] == 0), 0, jnp.maximum(slack, 0))
    passed = jax.random.randint(jax.random.fold_in(own, 4), (amount // 2,), 0, 1 << 20) % (slack + 1)
    sizes = sizes.at[giver].add(-passed).at[taker].add(passed)
    items = jnp.searchsorted(jnp.cumsum(sizes), jnp.arange(rows * top), side="right").astype(jnp.int32)
    listing = items.reshape(top, rows).T
    listing = listing[jax.random.permutation(jax.random.fold_in(own, 1), rows)]
    turn = jax.random.randint(jax.random.fold_in(own, 2), (rows, 1), 0, top)
    return jnp.take_along_axis(listing, (jnp.arange(top)[None, :] + turn) % top, axis=1)


def shares(count, total, most, lean, full):
    loads = [(1 << 20) // math.isqrt(standing ** lean) + 1 for standing in range(1, count + 1)]
    largest = most if full else min(most, max(-(-total // count), total * loads[0] // sum(loads)))
    least = 1 if total - largest >= count - 1 else 0
    given, rest = [largest] + [least] * (count - 1), total - largest - least * (count - 1)
    while rest > 0:
        movable = [i for i in range(1, count) if given[i] < largest] or [i for i in range(1, count) if given[i] < most]
        pool, left = sum([loads[i] for i in movable]), rest
        for i in movable:
            extra = min(most - given[i], max(1, left * loads[i] // pool), rest)
            given[i] = given[i] + extra
            rest = rest - extra
    return np.array(given)


def normal_values(stream_key, shape, width, most, cuts=(), kind=jnp.bfloat16):
    values = jax.random.normal(stream_key, shape, jnp.float32) * width
    if len(cuts) > 0:
        values = shard_levels(stream_key, shape, cuts, -0.22, 0.18) * values
    return jnp.clip(values, min=-most, max=most).astype(kind)


def setup_inputs(seed: int = 0) -> dict:
    key_list = jax.random.split(jax.random.key(seed), 16)
    q_nope = normal_values(key_list[0], (TOKENS, HEADS * NOPE), 1.0, 6.0, ((0, 32), (1, 4)))
    q_rope = draw_q_rope(jax.random.fold_in(key_list[15], 71), 0)
    w_absorb = normal_values(key_list[2], (HEADS, NOPE, LAT), NOPE ** -0.5, 0.5, ((0, 4),))
    cache_latent = normal_values(key_list[3], (REQS, LEN, LAT), 1.0, 6.0, ((0, 32),))
    cache_rope = draw_cache_rope(jax.random.fold_in(key_list[15], 71), 0)
    lengths = draw_lengths(jax.random.fold_in(key_list[15], 71), 0)
    w_value = normal_values(key_list[6], (HEADS, LAT, VDIM), (max(LAT // 64, 1)) ** -0.5, 2.0, ((0, 4),))
    w_out = normal_values(key_list[7], (HEADS * VDIM, D), (HEADS * VDIM) ** -0.5, 0.0625, ((0, 4), (1, 32)))
    residual = normal_values(key_list[8], (TOKENS, D), 1.0, 6.0, ((0, 32),))
    norm_gain = jnp.clip(1.0 + 0.1 * jax.random.normal(key_list[9], (D,), jnp.float32), 0.5, 1.5).astype(jnp.bfloat16)
    routes_keys = jax.random.split(jax.random.fold_in(key_list[10], 1), TOKENS // TOK_DEV)
    routes_turns = jax.random.permutation(jax.random.fold_in(key_list[10], 3), TOKENS // TOK_DEV)
    routes = jax.vmap(lambda own, number: assign_block(jax.random.fold_in(key_list[10], 2), own, number, TOK_DEV, EXPERTS, TOPK, CAP, 2))(routes_keys, routes_turns).reshape((TOKENS, TOPK))
    gate_int = plant(jax.random.randint(key_list[11], (TOKENS, TOPK), 1, 256), jax.random.fold_in(key_list[11], 1), 1, 255).astype(jnp.int32)
    w_gate = normal_values(key_list[12], (EXPERTS, D, FFE), D ** -0.5, 0.0625, ((0, 8), (2, 16)))
    w_up = normal_values(key_list[13], (EXPERTS, D, FFE), D ** -0.5, 0.0625, ((0, 8), (2, 16)))
    w_down = normal_values(key_list[14], (EXPERTS, FFE, D), FFE ** -0.5, 0.125, ((0, 8), (1, 16)))
    return dict(q_nope=q_nope, q_rope=q_rope, w_absorb=w_absorb, cache_latent=cache_latent, cache_rope=cache_rope, lengths=lengths, w_value=w_value, w_out=w_out, residual=residual, norm_gain=norm_gain, routes=routes, gate_int=gate_int, w_gate=w_gate, w_up=w_up, w_down=w_down)


EPS = 1e-06
ROUTE_SCALE = 2.5

def attend(item):
    q_latent, q_pos, latent, rotary, length = item
    scale = (NOPE + ROPE) ** (-0.5)
    scores = jnp.einsum('qhc,pc->qhp', q_latent.astype(jnp.float32), latent.astype(jnp.float32))
    scores = scores + jnp.einsum('qhe,ep->qhp', q_pos.astype(jnp.float32), rotary.astype(jnp.float32))
    scores = scores * scale
    position = jnp.arange(LEN, dtype=jnp.int32)
    limit = length - QPR + jnp.arange(QPR, dtype=jnp.int32)
    valid = position[None, None, :] <= limit[:, None, None]
    scores = jnp.where(valid, scores, -jnp.inf)
    top = lax.optimization_barrier(jnp.max(scores, axis=-1, keepdims=True))
    weights = jnp.exp(scores - top)
    probs = (weights / lax.optimization_barrier(jnp.sum(weights, axis=-1, keepdims=True))).astype(jnp.bfloat16)
    out = jnp.einsum('qhp,pc->qhc', probs.astype(jnp.float32), latent.astype(jnp.float32))
    return out.astype(jnp.bfloat16)

def reference(q_nope, q_rope, w_absorb, cache_latent, cache_rope, lengths, w_value, w_out, residual, norm_gain, routes, gate_int, w_gate, w_up, w_down):
    query = q_nope.reshape(TOKENS, HEADS, NOPE).astype(jnp.float32)
    q_latent = jnp.einsum('thn,hnc->thc', query, w_absorb.astype(jnp.float32)).astype(jnp.bfloat16)
    q_latent = q_latent.reshape(REQS, QPR, HEADS, LAT)
    q_pos = q_rope.reshape(REQS, QPR, HEADS, ROPE)
    latent_out = lax.map(attend, (q_latent, q_pos, cache_latent, cache_rope, lengths))
    latent_out = latent_out.reshape(TOKENS, HEADS, LAT)
    values = jnp.einsum('thc,hcv->thv', latent_out.astype(jnp.float32), w_value.astype(jnp.float32))
    values = values.astype(jnp.bfloat16).reshape(TOKENS, HEADS * VDIM)
    hidden = residual.astype(jnp.float32) + jnp.dot(values, w_out, preferred_element_type=jnp.float32)
    inverse = lax.rsqrt(lax.optimization_barrier(jnp.mean(hidden * hidden, axis=-1, keepdims=True)) + EPS)
    normed = (hidden * inverse * norm_gain.astype(jnp.float32)[None, :]).astype(jnp.bfloat16)
    gates = gate_int.astype(jnp.float32)
    gates = gates / lax.optimization_barrier(jnp.sum(gates, axis=1, keepdims=True))
    expert_ids = jnp.arange(EXPERTS, dtype=jnp.int32)
    hits = routes[:, :, None] == expert_ids[None, None, :]
    member = jnp.transpose(lax.optimization_barrier(jnp.sum(hits.astype(jnp.int32), axis=1))).astype(jnp.int32)
    weight = jnp.transpose(lax.optimization_barrier(jnp.sum(hits.astype(jnp.float32) * gates[:, :, None], axis=1)))
    rows = N_GRP * N_SIDE * CAP
    slots = jnp.arange(rows, dtype=jnp.int32)

    def step(total, item):
        gate_w, up_w, down_w, chosen_mask, chosen_weight = item
        rank = (jnp.cumsum(chosen_mask) - 1).astype(jnp.int32)
        pick = (rank[None, :] == slots[:, None]) & (chosen_mask[None, :] > 0)
        chosen = jnp.dot(pick.astype(jnp.bfloat16), normed, preferred_element_type=jnp.float32).astype(jnp.bfloat16)
        gate = jnp.dot(chosen, gate_w, preferred_element_type=jnp.float32)
        up = jnp.dot(chosen, up_w, preferred_element_type=jnp.float32)
        act = (jax.nn.silu(gate) * up).astype(jnp.bfloat16)
        out = jnp.dot(act, down_w, preferred_element_type=jnp.float32)
        spread = pick.astype(jnp.float32) * chosen_weight[None, :]
        return (total + jnp.dot(jnp.transpose(spread), out, precision=lax.Precision.HIGHEST), None)
    start = jnp.zeros((TOKENS, D), jnp.float32)
    total, unused = lax.scan(step, start, (w_gate, w_up, w_down, member, weight))
    moe = ROUTE_SCALE * total
    return (hidden + moe).astype(jnp.bfloat16)
```

```python
import jax
import jax.numpy as jnp
from jax import lax
from jax.experimental import pallas as pl
from jax.experimental.pallas import tpu as pltpu
from jax.sharding import Mesh
from jax.sharding import PartitionSpec as P

LAT = 512
ROPE = 64
NOPE = 128
VDIM = 128
QPR = 2
LEN = 4096
EPS = 1e-06
ROUTE_SCALE = 2.5
BF = jnp.bfloat16
F32 = jnp.float32

PAIRS_A = [(0, 1), (1, 0), (2, 3), (3, 2)]
PAIRS_B = [(1, 2), (2, 1), (3, 0), (0, 3)]
SWAP = [(0, 1), (1, 0)]


def attention(q_nope, q_rope, w_absorb, cache_latent, cache_rope, lengths, w_value):
    heads = w_absorb.shape[0]
    tok_rows = q_nope.shape[0]
    requests = cache_latent.shape[0]
    query = q_nope.reshape(tok_rows, heads, NOPE)
    q_latent = jnp.einsum("thn,hnc->thc", query, w_absorb, preferred_element_type=F32).astype(BF)
    q_latent = q_latent.reshape(requests, QPR, heads, LAT)
    q_pos = q_rope.reshape(requests, QPR, heads, ROPE)
    scale = (NOPE + ROPE) ** (-0.5)
    scores = jnp.einsum("rqhc,rpc->rqhp", q_latent, cache_latent, preferred_element_type=F32)
    scores = scores + jnp.einsum("rqhe,rep->rqhp", q_pos, cache_rope, preferred_element_type=F32)
    scores = scores * scale
    position = jnp.arange(LEN, dtype=jnp.int32)
    limit = lengths[:, None] - QPR + jnp.arange(QPR, dtype=jnp.int32)[None, :]
    valid = position[None, None, None, :] <= limit[:, :, None, None]
    scores = jnp.where(valid, scores, -jnp.inf)
    top = jnp.max(scores, axis=-1, keepdims=True)
    weights = jnp.exp(scores - top)
    probs = (weights / jnp.sum(weights, axis=-1, keepdims=True)).astype(BF)
    latent_out = jnp.einsum("rqhp,rpc->rqhc", probs, cache_latent, preferred_element_type=F32).astype(BF)
    latent_out = latent_out.reshape(tok_rows, heads, LAT)
    values = jnp.einsum("thc,hcv->thv", latent_out, w_value, preferred_element_type=F32).astype(BF)
    return values.reshape(tok_rows, heads * VDIM)


def ffn_kernel(own_ref, oth_ref, gain_ref, share_ref, wg_hbm, wu_hbm, wd_hbm, keep_ref, send_ref,
               wgu, wd, sem_up, sem_down):
    experts, depth, units = wg_hbm.shape
    blocks, rows, cols = own_ref.shape
    sides = 4
    ys = blocks // sides
    stripe = depth // ys
    half = rows // 2
    core = lax.axis_index("c")
    copies = []
    for y in range(ys):
        group = []
        for e in range(experts):
            for k, src in enumerate((wg_hbm, wu_hbm)):
                group.append(pltpu.make_async_copy(
                    src.at[e, pl.ds(y * stripe, stripe), :],
                    wgu.at[e, pl.ds(y * stripe, stripe), pl.ds(k * units, units)],
                    sem_up.at[(y * experts + e) * 2 + k],
                ))
        copies.append(group)
    downs = [
        pltpu.make_async_copy(wd_hbm.at[e], wd.at[pl.ds(e * units, units), :], sem_down.at[e])
        for e in range(experts)
    ]
    for group in copies:
        for copy in group:
            copy.start()
    for copy in downs:
        copy.start()
    acc = [jnp.zeros((rows, 2 * units), F32) for _ in range(experts)]
    square = jnp.zeros((rows, cols), F32)
    for y in range(ys):
        for copy in copies[y]:
            copy.wait()
        for other in range(2):
            part = core if other == 0 else 1 - core
            for s in range(sides):
                if other == 0:
                    block = own_ref[y * sides + s].astype(F32)
                else:
                    block = oth_ref[y * sides + s].astype(F32)
                    block = jnp.concatenate([block[half:], block[:half]], axis=0)
                square = square + block * block
                scaled = (block * gain_ref[y * 2 + part, pl.ds(s, 1), :]).astype(BF)
                start = pl.multiple_of(y * stripe + part * (stripe // 2) + s * cols, 16)
                for e in range(experts):
                    acc[e] = acc[e] + jnp.dot(scaled, wgu[e, pl.ds(start, cols), :], preferred_element_type=F32)
    inverse = lax.rsqrt(jnp.sum(square, axis=-1, keepdims=True) / depth + EPS)
    acts = []
    for e in range(experts):
        both = acc[e] * inverse
        gate, up = both[:, :units], both[:, units:]
        share = share_ref[:, e:e + 1]
        act = gate / (1.0 + jnp.exp(-gate)) * up
        acts.append(jnp.where(share > 0, act * share, 0.0).astype(BF))
    act = jnp.concatenate(acts, axis=1)
    for copy in downs:
        copy.wait()
    tile = 1024
    for n in range(depth // tile):
        out = jnp.dot(act, wd[:, n * tile:(n + 1) * tile], preferred_element_type=F32).astype(BF)
        keep_ref[:, n * tile:(n + 1) * tile] = out[:half]
        send_ref[:, n * tile:(n + 1) * tile] = out[half:]


def ffn(own, oth, gain, share, w_gate, w_up, w_down):
    experts, depth, units = w_gate.shape
    rows = own.shape[1]
    shape = jax.ShapeDtypeStruct((rows // 2, depth), BF)
    return pl.pallas_call(
        ffn_kernel,
        out_shape=(shape, shape),
        in_specs=[pl.BlockSpec(memory_space=pltpu.VMEM)] * 4 + [pl.BlockSpec(memory_space=pl.ANY)] * 3,
        out_specs=[pl.BlockSpec(memory_space=pltpu.VMEM)] * 2,
        scratch_shapes=[
            pltpu.VMEM((experts, depth, 2 * units), BF),
            pltpu.VMEM((experts * units, depth), BF),
            pltpu.SemaphoreType.DMA((16,)),
            pltpu.SemaphoreType.DMA((2,)),
        ],
        compiler_params=pltpu.CompilerParams(vmem_limit_bytes=40 * 1024 * 1024),
        cost_estimate=pl.CostEstimate(flops=2 * rows * depth * 768, bytes_accessed=15_000_000, transcendentals=0),
    )(own, oth, gain, share, w_gate, w_up, w_down)


def body(
    q_nope, q_rope, w_absorb, cache_latent, cache_rope, lengths, w_value, w_out, residual, norm_gain,
    routes, gate_int, w_gate, w_up, w_down,
):
    hgs, ys, cores, sides = (lax.axis_size(a) for a in ("hg", "y", "c", "side"))
    hg, y, core, side = (lax.axis_index(a) for a in ("hg", "y", "c", "side"))
    planes = ys * sides
    toks, width = residual.shape
    cols = w_out.shape[1]
    local_experts = w_gate.shape[0]
    experts_all = local_experts * ys * cores

    values = attention(q_nope, q_rope, w_absorb, cache_latent, cache_rope, lengths, w_value)

    expert_ids = jnp.arange(experts_all, dtype=jnp.int32)
    hits = routes[:, :, None] == expert_ids[None, None, :]
    dense = jnp.sum(jnp.where(hits, gate_int[:, :, None], 0), axis=1).astype(BF)
    row = lax.dynamic_slice_in_dim(residual, hg, 1, 0)
    row = row.reshape(ys, cores, sides, cols).transpose(0, 2, 1, 3).reshape(planes, cores * 2, cols // 2)
    message = jnp.concatenate(
        [
            jnp.broadcast_to(values[None], (planes,) + values.shape),
            row,
            jnp.broadcast_to(dense[None], (planes,) + dense.shape),
        ],
        axis=2,
    )
    here = lax.all_to_all(message, ("y", "side"), 0, 0, tiled=True)
    there = lax.ppermute(here, "c", SWAP)
    both = jnp.stack([here, there])
    n_val = values.shape[1]
    all_values = both[..., :n_val].reshape(cores * planes * toks, n_val)
    extra = both[..., n_val:]
    mine = lax.dynamic_slice_in_dim(extra[..., :cols // 2], core * 2, 2, 2).reshape(cores * planes, 1, cols)
    gates = extra[..., cols // 2:].reshape(cores * planes * toks, experts_all).astype(F32)
    total = jnp.sum(gates, axis=1, keepdims=True)
    first = (y * cores + core) * local_experts
    share = lax.dynamic_slice_in_dim(gates, first, local_experts, 1) * (ROUTE_SCALE / total)

    partial = jnp.dot(all_values, w_out, preferred_element_type=F32).reshape(cores * planes, toks, cols)
    is_row = (jnp.arange(toks) == hg)[None, :, None]
    partial = (partial + jnp.where(is_row, mine.astype(F32), 0.0)).astype(BF).reshape(-1, cols)
    pair = (partial.astype(F32) + lax.ppermute(partial, "hg", PAIRS_A).astype(F32)).astype(BF)
    hidden = (pair.astype(F32) + lax.ppermute(pair, "hg", PAIRS_B).astype(F32)).astype(BF)

    own = lax.all_to_all(jnp.broadcast_to(hidden[None], (planes,) + hidden.shape), ("y", "side"), 0, 0, tiled=True)
    oth = lax.ppermute(own, "c", SWAP)
    gain = norm_gain.astype(F32).reshape(ys * cores, sides, cols)
    keep, send = ffn(own, oth, gain, share, w_gate, w_up, w_down)
    got = lax.ppermute(send, "c", SWAP)
    quarter = width // hgs
    summed = (keep.astype(F32) + got.astype(F32)).astype(BF)
    summed = summed.reshape(planes, toks, hgs, quarter).transpose(2, 0, 1, 3).reshape(hgs * planes, toks, quarter)
    parts = lax.all_to_all(summed, ("hg", "y", "side"), 0, 0, tiled=True)

    at = (y * sides + side) * toks
    half = planes * toks
    first_half = lax.dynamic_slice(own, (hg * sides, at, 0), (sides, toks, cols))
    second_half = lax.dynamic_slice(oth, (hg * sides, half + at, 0), (sides, toks, cols))
    low = jnp.where(core == 0, first_half, second_half)
    high = jnp.where(core == 0, second_half, first_half)
    kept = jnp.concatenate([low, high], axis=0).transpose(1, 0, 2).reshape(toks, quarter)
    return (kept.astype(F32) + jnp.sum(parts.astype(F32), axis=0)).astype(BF)


def solution(mesh):
    devices = mesh.devices
    fine = Mesh(devices.reshape(4, 4, 2, 4), ("hg", "y", "c", "side"))
    grp = ("y", "c")
    plane = ("y", "c", "side")
    in_specs = (
        P(plane, "hg"),
        P(plane, "hg"),
        P("hg", None, None),
        P(plane, None, None),
        P(plane, None, None),
        P(plane),
        P("hg", None, None),
        P("hg", plane),
        P(plane, None),
        P(),
        P(plane, None),
        P(plane, None),
        P(grp, None, ("hg", "side")),
        P(grp, None, ("hg", "side")),
        P(grp, ("hg", "side"), None),
    )
    return jax.shard_map(body, mesh=fine, in_specs=in_specs, out_specs=P(plane, "hg"), check_vma=False)
```

```python
import functools

import jax
import jax.numpy as jnp
from jax import lax
from jax.experimental import pallas as pl
from jax.experimental.pallas import tpu as pltpu
from jax.sharding import Mesh
from jax.sharding import PartitionSpec as P

LAT = 512
ROPE = 64
NOPE = 128
VDIM = 128
QPR = 2
LEN = 4096
EPS = 1e-06
ROUTE_SCALE = 2.5
BF = jnp.bfloat16
F32 = jnp.float32

PAIRS_A = [(0, 1), (1, 0), (2, 3), (3, 2)]
PAIRS_B = [(1, 2), (2, 1), (3, 0), (0, 3)]
SWAP = [(0, 1), (1, 0)]


def attention_kernel(len_ref, qn_ref, qr_ref, res_ref, routes_ref, ints_ref, wa_hbm, lat_hbm, rope_hbm, wv_hbm, out_ref,
                     wa, wv, lat, rope, qs, qps, os, ext, sem_w, sem_l, sem_r, *, span, sides, experts):
    reqs, length, width = lat_hbm.shape
    heads = wa_hbm.shape[0]
    toks = qn_ref.shape[0]
    qpr = toks // reqs
    rows = qpr * heads
    spans = length // span
    lanes = width // 128
    scale = (NOPE + ROPE) ** (-0.5)
    absorb = pltpu.make_async_copy(wa_hbm, wa, sem_w.at[0])
    absorb.start()
    value = pltpu.make_async_copy(wv_hbm, wv, sem_w.at[1])

    def copies(r, i):
        at = pl.ds(i * span, span)
        return (
            pltpu.make_async_copy(lat_hbm.at[r, at, :], lat.at[r, at, :], sem_l.at[r * spans + i]),
            pltpu.make_async_copy(rope_hbm.at[r, :, at], rope.at[r, :, at], sem_r.at[r * spans + i]),
        )

    for r in range(reqs):
        for i in range(spans):
            def begin(r=r, i=i):
                for copy in copies(r, i):
                    copy.start()

            if i == 0:
                begin()
            else:
                pl.when(i * span < len_ref[r])(begin)
    value.start()
    planes = out_ref.shape[0]
    cores = 2
    n_val = heads * VDIM
    cols = res_ref.shape[1] // (planes * cores)
    which = lax.broadcasted_iota(jnp.int32, res_ref.shape, 0) == lax.axis_index("hg")
    row = jnp.sum(jnp.where(which, res_ref[...].astype(F32), 0.0), axis=0, keepdims=True)
    lane = lax.broadcasted_iota(jnp.int32, (1, 128), 1)
    dense = jnp.zeros((1, 128), jnp.int32)
    for j in range(toks):
        for k in range(routes_ref.shape[1]):
            dense = dense + jnp.where(lane == j * experts + routes_ref[j, k], ints_ref[j, k], 0)
    dense = dense.astype(F32)
    for p in range(planes):
        y, side = divmod(p, sides)
        for c in range(cores):
            start = ((y * cores + c) * sides + side) * cols // 128
            for t in range(3):
                tile = min(start + t, res_ref.shape[1] // 128 - 1)
                ext[p, pl.ds(t, 1), c * 128:(c + 1) * 128] = row[:, tile * 128:(tile + 1) * 128]
        ext[p, pl.ds(3, 1), :] = jnp.concatenate([dense, dense], axis=1)
    for p in range(planes):
        out_ref[p, :, n_val:] = ext[p].astype(BF)
    turned = qr_ref[...].astype(F32)
    for h in range(heads):
        pair = turned[:, (h // 2) * 2 * ROPE:(h // 2 + 1) * 2 * ROPE]
        if h % 2:
            pair = jnp.concatenate([pair[:, ROPE:], pair[:, :ROPE]], axis=1)
        qps[pl.ds(h, toks, stride=heads), :] = pair
    absorb.wait()
    for h in range(heads):
        latent = jnp.dot(qn_ref[:, h * NOPE:(h + 1) * NOPE], wa[h], preferred_element_type=F32)
        for c in range(lanes):
            qs[c, pl.ds(h, toks, stride=heads), :] = latent[:, c * 128:(c + 1) * 128]
    for r in range(reqs):
        at = pl.ds(r * rows, rows)
        query = jnp.concatenate([qs[c, at, :] for c in range(lanes)], axis=1).astype(BF)
        rotary = qps[at, :ROPE].astype(BF)
        filled = len_ref[r]
        limit = filled - qpr + lax.broadcasted_iota(jnp.int32, (rows, 1), 0) // heads

        def step(i, old, r=r, query=query, rotary=rotary, limit=limit):
            for copy in copies(r, i):
                copy.wait()
            keys = lat[r, pl.ds(i * span, span), :]
            s = lax.dot_general(query, keys, (((1,), (1,)), ((), ())), preferred_element_type=F32)
            s = s + jnp.dot(rotary, rope[r, :, pl.ds(i * span, span)], preferred_element_type=F32)
            position = i * span + lax.broadcasted_iota(jnp.int32, (rows, span), 1)
            s = jnp.where(position <= limit, s * scale, -jnp.inf)
            top = jnp.max(s, axis=1, keepdims=True)
            if old is not None:
                top = jnp.maximum(old[0], top)
            p = jnp.exp(s - top)
            norm = jnp.sum(p, axis=1, keepdims=True)
            acc = jnp.dot(p.astype(BF), keys, preferred_element_type=F32)
            if old is not None:
                fade = jnp.exp(old[0] - top)
                norm = norm + fade * old[1]
                acc = acc + fade * old[2]
            return top, norm, acc

        state = step(0, None)
        for i in range(1, spans):
            state = lax.cond(i * span < filled, functools.partial(step, i), lambda old: old, state)
        result = state[2] / state[1]
        for c in range(lanes):
            os[c, at, :] = result[:, c * 128:(c + 1) * 128]
    value.wait()
    for h in range(heads):
        at = pl.ds(h, toks, stride=heads)
        o = jnp.concatenate([os[c, at, :] for c in range(lanes)], axis=1).astype(BF)
        head = jnp.dot(o, wv[h], preferred_element_type=F32).astype(BF)
        for k in range(planes):
            out_ref[k, :, h * VDIM:(h + 1) * VDIM] = head


def attention(q_nope, q_rope, w_absorb, cache_latent, cache_rope, lengths, w_value, residual, routes, gate_int,
              planes, sides, experts, span=2048):
    reqs, length, width = cache_latent.shape
    spans = length // span
    heads = w_absorb.shape[0]
    toks = q_nope.shape[0]
    hbm = pl.BlockSpec(memory_space=pltpu.HBM)
    vmem = pl.BlockSpec(memory_space=pltpu.VMEM)
    smem = pl.BlockSpec(memory_space=pltpu.SMEM)
    return pl.pallas_call(
        functools.partial(attention_kernel, span=span, sides=sides, experts=experts),
        out_shape=jax.ShapeDtypeStruct((planes, toks, heads * VDIM + 256), BF),
        in_specs=[smem] + [vmem] * 3 + [smem] * 2 + [hbm] * 4,
        out_specs=vmem,
        scratch_shapes=[
            pltpu.VMEM(w_absorb.shape, BF),
            pltpu.VMEM(w_value.shape, BF),
            pltpu.VMEM(cache_latent.shape, BF),
            pltpu.VMEM(cache_rope.shape, BF),
            pltpu.VMEM((width // 128, toks * heads, 128), F32),
            pltpu.VMEM((toks * heads, 2 * ROPE), F32),
            pltpu.VMEM((width // 128, toks * heads, 128), F32),
            pltpu.VMEM((planes, toks, 256), F32),
            pltpu.SemaphoreType.DMA((2,)),
            pltpu.SemaphoreType.DMA((reqs * spans,)),
            pltpu.SemaphoreType.DMA((reqs * spans,)),
        ],
        compiler_params=pltpu.CompilerParams(vmem_limit_bytes=60 * 1024 * 1024),
        name="attention",
    )(lengths, q_nope, q_rope, residual, routes, gate_int, w_absorb, cache_latent, cache_rope, w_value)


def half_copies(wg_hbm, wu_hbm, wg, wu, sem, part, stripes):
    experts, depth, _ = wg_hbm.shape
    stripe = depth // stripes
    half = stripe // 2
    groups = []
    for y in range(stripes):
        at = pl.ds(pl.multiple_of(y * stripe + part * half, 16), half)
        to = pl.ds(y * half, half)
        groups.append([
            pltpu.make_async_copy(src.at[e, at, :], dst.at[e, to, :], sem.at[(y * experts + e) * 2 + k])
            for e in range(experts)
            for k, (src, dst) in enumerate(((wg_hbm, wg), (wu_hbm, wu)))
        ])
    return groups


def half_products(blocks_ref, gain_ref, wg, wu, groups, part, acc, swap):
    blocks, rows, _ = blocks_ref.shape
    stripes = len(groups)
    sides = blocks // stripes
    cols = gain_ref.shape[2]
    half = rows // 2
    square = jnp.zeros((rows, cols), F32)
    for y in range(stripes):
        for copy in groups[y]:
            copy.wait()
        for s in range(sides):
            block = blocks_ref[y * sides + s, :, :cols].astype(F32)
            if swap:
                block = jnp.concatenate([block[half:], block[:half]], axis=0)
            square = square + block * block
            scaled = (block * gain_ref[y * 2 + part, pl.ds(s, 1), :]).astype(BF)
            at = pl.ds((y * sides + s) * cols, cols)
            for e in range(len(acc)):
                both = jnp.concatenate([wg[e, at, :], wu[e, at, :]], axis=1)
                acc[e] = acc[e] + jnp.dot(scaled, both, preferred_element_type=F32)
    return acc, jnp.sum(square, axis=-1, keepdims=True)


def first_kernel(own_ref, gain_ref, wg_hbm, wu_hbm, acc_ref, sq_ref, wg, wu, sem):
    experts, depth, units = wg_hbm.shape
    rows = own_ref.shape[1]
    core = lax.axis_index("c")
    groups = half_copies(wg_hbm, wu_hbm, wg, wu, sem, core, gain_ref.shape[0] // 2)
    for group in groups:
        for copy in group:
            copy.start()
    acc = [jnp.zeros((rows, 2 * units), F32) for _ in range(experts)]
    acc, square = half_products(own_ref, gain_ref, wg, wu, groups, core, acc, False)
    for e in range(experts):
        acc_ref[e] = acc[e]
    sq_ref[...] = square


def second_kernel(oth_ref, gain_ref, share_ref, acc_ref, sq_ref, wg_hbm, wu_hbm, wd_hbm, keep_ref, send_ref,
                  wg, wu, wd, sem, sem_down):
    experts, depth, units = wg_hbm.shape
    blocks, rows, _ = oth_ref.shape
    half = rows // 2
    part = 1 - lax.axis_index("c")
    groups = half_copies(wg_hbm, wu_hbm, wg, wu, sem, part, gain_ref.shape[0] // 2)
    downs = [
        pltpu.make_async_copy(wd_hbm.at[e], wd.at[pl.ds(e * units, units), :], sem_down.at[e])
        for e in range(experts)
    ]
    for group in groups:
        for copy in group:
            copy.start()
    for copy in downs:
        copy.start()
    acc, square = half_products(oth_ref, gain_ref, wg, wu, groups, part, [acc_ref[e] for e in range(experts)], True)
    inverse = lax.rsqrt((square + sq_ref[...]) / depth + EPS)
    acts = []
    for e in range(experts):
        both = acc[e] * inverse
        gate, up = both[:, :units], both[:, units:]
        share = share_ref[:, e:e + 1]
        act = gate / (1.0 + jnp.exp(-gate)) * up
        acts.append(jnp.where(share > 0, act * share, 0.0).astype(BF))
    act = jnp.concatenate(acts, axis=1)
    for copy in downs:
        copy.wait()
    messages, lines, tile = keep_ref.shape
    toks = lines // 2
    for n in range(depth // (2 * tile)):
        left = jnp.dot(act, wd[:, 2 * n * tile:(2 * n + 1) * tile], preferred_element_type=F32)
        right = jnp.dot(act, wd[:, (2 * n + 1) * tile:(2 * n + 2) * tile], preferred_element_type=F32)
        for k in range(blocks):
            for ref, base in ((keep_ref, 0), (send_ref, half)):
                at = slice(base + k * toks, base + (k + 1) * toks)
                ref[n * blocks + k] = jnp.concatenate([left[at], right[at]], axis=0).astype(BF)


def own_half(own, gain, w_gate, w_up):
    experts, depth, units = w_gate.shape
    rows = own.shape[1]
    vmem = pl.BlockSpec(memory_space=pltpu.VMEM)
    hbm = pl.BlockSpec(memory_space=pltpu.HBM)
    w_gate, w_up = (pltpu.with_memory_space_constraint(a, pltpu.HBM) for a in (w_gate, w_up))
    return pl.pallas_call(
        first_kernel,
        out_shape=(jax.ShapeDtypeStruct((experts, rows, 2 * units), F32), jax.ShapeDtypeStruct((rows, 1), F32)),
        in_specs=[vmem] * 2 + [hbm] * 2,
        out_specs=[vmem] * 2,
        scratch_shapes=[
            pltpu.VMEM((experts, depth // 2, units), BF),
            pltpu.VMEM((experts, depth // 2, units), BF),
            pltpu.SemaphoreType.DMA((gain.shape[0] * experts,)),
        ],
        compiler_params=pltpu.CompilerParams(vmem_limit_bytes=16 * 1024 * 1024),
        cost_estimate=pl.CostEstimate(flops=rows * depth * 512, bytes_accessed=5_000_000, transcendentals=0),
        name="experts_first",
    )(own, gain, w_gate, w_up)


def other_half(oth, gain, share, acc, square, w_gate, w_up, w_down, hgs):
    experts, depth, units = w_gate.shape
    blocks, rows, _ = oth.shape
    shape = jax.ShapeDtypeStruct((hgs * blocks, rows // blocks, depth // hgs // 2), BF)
    vmem = pl.BlockSpec(memory_space=pltpu.VMEM)
    hbm = pl.BlockSpec(memory_space=pltpu.HBM)
    w_gate, w_up, w_down = (pltpu.with_memory_space_constraint(a, pltpu.HBM) for a in (w_gate, w_up, w_down))
    return pl.pallas_call(
        second_kernel,
        out_shape=(shape, shape),
        in_specs=[vmem] * 5 + [hbm] * 3,
        out_specs=[vmem] * 2,
        scratch_shapes=[
            pltpu.VMEM((experts, depth // 2, units), BF),
            pltpu.VMEM((experts, depth // 2, units), BF),
            pltpu.VMEM((experts * units, depth), BF),
            pltpu.SemaphoreType.DMA((gain.shape[0] * experts,)),
            pltpu.SemaphoreType.DMA((experts,)),
        ],
        compiler_params=pltpu.CompilerParams(vmem_limit_bytes=24 * 1024 * 1024),
        cost_estimate=pl.CostEstimate(flops=rows * depth * 1024, bytes_accessed=10_000_000, transcendentals=0),
        name="experts_second",
    )(oth, gain, share, acc, square, w_gate, w_up, w_down)


def body(
    q_nope, q_rope, w_absorb, cache_latent, cache_rope, lengths, w_value, w_out, residual, norm_gain,
    routes, gate_int, w_gate, w_up, w_down,
):
    hgs, ys, cores, sides = (lax.axis_size(a) for a in ("hg", "y", "c", "side"))
    hg, y, core, side = (lax.axis_index(a) for a in ("hg", "y", "c", "side"))
    planes = ys * sides
    toks, width = residual.shape
    cols = w_out.shape[1]
    local_experts = w_gate.shape[0]
    experts_all = local_experts * ys * cores

    message = attention(q_nope, q_rope, w_absorb, cache_latent, cache_rope, lengths, w_value, residual, routes, gate_int,
                        planes, sides, experts_all)
    here = lax.all_to_all(message, ("y", "side"), 0, 0, tiled=True)
    there = lax.ppermute(here, "c", SWAP)
    both = jnp.stack([here, there])
    n_val = w_absorb.shape[0] * VDIM
    all_values = both[..., :n_val].reshape(cores * planes * toks, n_val)
    extra = both[..., n_val:]
    window = lax.dynamic_slice_in_dim(extra[..., :3, :], core * 128, 128, 3).reshape(cores * planes, 3 * 128)
    block = (y * cores + core) * sides + side
    mine = lax.dynamic_slice_in_dim(window, lax.rem(block * cols, 128), cols, 1)[:, None]
    gates = extra[..., 3, :toks * experts_all].reshape(cores * planes * toks, experts_all).astype(F32)
    total = jnp.sum(gates, axis=1, keepdims=True)
    first = (y * cores + core) * local_experts
    share = lax.dynamic_slice_in_dim(gates, first, local_experts, 1) * (ROUTE_SCALE / total)

    partial = jnp.dot(all_values, w_out, preferred_element_type=F32).reshape(cores * planes, toks, cols)
    is_row = (jnp.arange(toks) == hg)[None, :, None]
    partial = (partial + jnp.where(is_row, mine.astype(F32), 0.0)).astype(BF).reshape(-1, cols)
    partial = jnp.pad(partial, ((0, 0), (0, -cols % 128)))
    pair = (partial.astype(F32) + lax.ppermute(partial, "hg", PAIRS_A).astype(F32)).astype(BF)
    hidden = (pair.astype(F32) + lax.ppermute(pair, "hg", PAIRS_B).astype(F32)).astype(BF)

    own = lax.all_to_all(jnp.broadcast_to(hidden[None], (planes,) + hidden.shape), ("y", "side"), 0, 0, tiled=True)
    oth = lax.ppermute(own, "c", SWAP)
    gain = norm_gain.astype(F32).reshape(ys * cores, sides, cols)
    acc, square = own_half(own, gain, w_gate, w_up)
    keep, send = other_half(oth, gain, share, acc, square, w_gate, w_up, w_down, hgs)
    got = lax.ppermute(send, "c", SWAP)
    quarter = width // hgs
    summed = keep + got
    at = (y * sides + side) * toks
    half = planes * toks
    own_piece = lax.dynamic_slice(own, (hg * sides, at, 0), (sides, toks, cols))
    oth_piece = lax.dynamic_slice(oth, (hg * sides, half + at, 0), (sides, toks, cols))
    low = jnp.where(core == 0, own_piece, oth_piece)
    high = jnp.where(core == 0, oth_piece, own_piece)
    kept = jnp.concatenate([low, high], axis=0).transpose(1, 0, 2).reshape(toks, quarter)
    summed, kept = lax.optimization_barrier((summed, kept))
    parts = lax.all_to_all(summed, ("hg", "y", "side"), 0, 0, tiled=True)
    moe = jnp.sum(parts.astype(F32), axis=0)
    moe = jnp.concatenate([moe[:toks], moe[toks:]], axis=1)
    return (kept.astype(F32) + moe).astype(BF)


def solution(mesh):
    devices = mesh.devices
    fine = Mesh(devices.reshape(4, 4, 2, 4), ("hg", "y", "c", "side"))
    grp = ("y", "c")
    plane = ("y", "c", "side")
    in_specs = (
        P(plane, "hg"),
        P(plane, "hg"),
        P("hg", None, None),
        P(plane, None, None),
        P(plane, None, None),
        P(plane),
        P("hg", None, None),
        P("hg", plane),
        P(plane, None),
        P(),
        P(plane, None),
        P(plane, None),
        P(grp, None, ("hg", "side")),
        P(grp, None, ("hg", "side")),
        P(grp, ("hg", "side"), None),
    )
    return jax.shard_map(body, mesh=fine, in_specs=in_specs, out_specs=P(plane, "hg"), check_vma=False)
```

```python
import functools

import jax
import jax.numpy as jnp
from jax import lax
from jax.experimental import pallas as pl
from jax.experimental.pallas import tpu as pltpu
from jax.sharding import Mesh
from jax.sharding import PartitionSpec as P

LAT = 512
ROPE = 64
NOPE = 128
VDIM = 128
QPR = 2
LEN = 4096
EPS = 1e-06
ROUTE_SCALE = 2.5
BF = jnp.bfloat16
F32 = jnp.float32

PAIRS_A = [(0, 1), (1, 0), (2, 3), (3, 2)]
PAIRS_B = [(1, 2), (2, 1), (3, 0), (0, 3)]
SWAP = [(0, 1), (1, 0)]


def attention_kernel(len_hbm, routes_hbm, ints_hbm, qn_hbm, qr_hbm, res_hbm, wa_hbm, lat_hbm, rope_hbm, wv_hbm, out_ref,
                     len_ref, routes_ref, ints_ref, qn_ref, qr_ref, res_ref, sem_in, wa, wv, lat, rope, qs, qps, os, ext, sc, sem_w, sem_l, sem_r, *, span, ahead, sides, experts):
    reqs, length, width = lat_hbm.shape
    heads = wa_hbm.shape[0]
    toks = qn_hbm.shape[0]
    qpr = toks // reqs
    rows = qpr * heads
    spans = length // span
    lanes = width // 128
    scale = (NOPE + ROPE) ** (-0.5)
    absorb = pltpu.make_async_copy(wa_hbm, wa, sem_w.at[0])
    small = [
        pltpu.make_async_copy(a, b, sem_in.at[k])
        for k, (a, b) in enumerate((
            (len_hbm, len_ref), (routes_hbm, routes_ref), (ints_hbm, ints_ref),
            (qn_hbm, qn_ref), (qr_hbm, qr_ref), (res_hbm, res_ref),
        ))
    ]
    for copy in small:
        copy.start()
    absorb.start()
    value = pltpu.make_async_copy(wv_hbm, wv, sem_w.at[1])

    def copies(r, i):
        at = pl.ds(i * span, span)
        return (
            pltpu.make_async_copy(lat_hbm.at[r, at, :], lat.at[r, at, :], sem_l.at[r * spans + i]),
            pltpu.make_async_copy(rope_hbm.at[r, :, at], rope.at[r, :, at], sem_r.at[r * spans + i]),
        )

    chunks = [(r, i) for r in range(reqs) for i in range(spans)]

    def begin(k):
        if k == len(chunks):
            value.start(priority=1)
        elif k < len(chunks):
            r, i = chunks[k]

            def go():
                for copy in copies(r, i):
                    copy.start(priority=1)

            if i == 0:
                go()
            else:
                pl.when(i * span < len_ref[r])(go)

    begin(0)
    for copy in small:
        copy.wait()
    for k in range(1, ahead):
        begin(k)
    planes = out_ref.shape[0]
    cores = 2
    n_val = heads * VDIM
    cols = res_ref.shape[1] // (planes * cores)
    which = lax.broadcasted_iota(jnp.int32, res_ref.shape, 0) == lax.axis_index("hg")
    row = jnp.sum(jnp.where(which, res_ref[...].astype(F32), 0.0), axis=0, keepdims=True)
    lane = lax.broadcasted_iota(jnp.int32, (1, 128), 1)
    dense = jnp.zeros((1, 128), jnp.int32)
    for j in range(toks):
        for k in range(routes_ref.shape[1]):
            dense = dense + jnp.where(lane == j * experts + routes_ref[j, k], ints_ref[j, k], 0)
    dense = dense.astype(F32)
    for p in range(planes):
        y, side = divmod(p, sides)
        for c in range(cores):
            start = ((y * cores + c) * sides + side) * cols // 128
            for t in range(3):
                tile = min(start + t, res_ref.shape[1] // 128 - 1)
                ext[p, pl.ds(t, 1), c * 128:(c + 1) * 128] = row[:, tile * 128:(tile + 1) * 128]
        ext[p, pl.ds(3, 1), :] = jnp.concatenate([dense, dense], axis=1)
    for p in range(planes):
        out_ref[p, :, n_val:] = ext[p].astype(BF)
    turned = qr_ref[...].astype(F32)
    for h in range(heads):
        pair = turned[:, (h // 2) * 2 * ROPE:(h // 2 + 1) * 2 * ROPE]
        if h % 2:
            pair = jnp.concatenate([pair[:, ROPE:], pair[:, :ROPE]], axis=1)
        qps[pl.ds(h, toks, stride=heads), :] = pair
    absorb.wait()
    for h in range(heads):
        latent = jnp.dot(qn_ref[:, h * NOPE:(h + 1) * NOPE], wa[h], preferred_element_type=F32)
        for c in range(lanes):
            qs[c, pl.ds(h, toks, stride=heads), :] = latent[:, c * 128:(c + 1) * 128]
    for r in range(reqs):
        at = pl.ds(r * rows, rows)
        query = jnp.concatenate([qs[c, at, :] for c in range(lanes)], axis=1).astype(BF)
        rotary = qps[at, :ROPE].astype(BF)
        filled = len_ref[r]
        limit = filled - qpr + lax.broadcasted_iota(jnp.int32, (rows, 1), 0) // heads
        for i in range(spans):
            begin(r * spans + i + ahead)
            to = pl.ds(i * span, span)

            def score(r=r, i=i, to=to, query=query, rotary=rotary):
                for copy in copies(r, i):
                    copy.wait()
                s = lax.dot_general(query, lat[r, to, :], (((1,), (1,)), ((), ())), preferred_element_type=F32)
                sc[:, to] = (s + jnp.dot(rotary, rope[r, :, to], preferred_element_type=F32)) * scale

            if i == 0:
                score()
            else:
                pl.when(i * span < filled)(score)
        position = lax.broadcasted_iota(jnp.int32, (rows, length), 1)
        s = jnp.where(position <= limit, sc[...], -jnp.inf)
        p = jnp.exp(s - jnp.max(s, axis=1, keepdims=True))
        norm = jnp.sum(p, axis=1, keepdims=True)
        p = p.astype(BF)
        acc = jnp.dot(p[:, :span], lat[r, pl.ds(0, span), :], preferred_element_type=F32)
        for i in range(1, spans):
            def add(old, r=r, i=i, p=p):
                return old + jnp.dot(p[:, i * span:(i + 1) * span], lat[r, pl.ds(i * span, span), :],
                                     preferred_element_type=F32)

            acc = lax.cond(i * span < filled, add, lambda old: old, acc)
        result = acc / norm
        for c in range(lanes):
            os[c, at, :] = result[:, c * 128:(c + 1) * 128]
    value.wait()
    for h in range(heads):
        at = pl.ds(h, toks, stride=heads)
        o = jnp.concatenate([os[c, at, :] for c in range(lanes)], axis=1).astype(BF)
        head = jnp.dot(o, wv[h], preferred_element_type=F32).astype(BF)
        for k in range(planes):
            out_ref[k, :, h * VDIM:(h + 1) * VDIM] = head


def attention(q_nope, q_rope, w_absorb, cache_latent, cache_rope, lengths, w_value, residual, routes, gate_int,
              planes, sides, experts, span=2048, ahead=5):
    reqs, length, width = cache_latent.shape
    spans = length // span
    heads = w_absorb.shape[0]
    toks = q_nope.shape[0]
    hbm = pl.BlockSpec(memory_space=pltpu.HBM)
    vmem = pl.BlockSpec(memory_space=pltpu.VMEM)
    return pl.pallas_call(
        functools.partial(attention_kernel, span=span, ahead=ahead, sides=sides, experts=experts),
        out_shape=pltpu.VMEM((planes, toks, heads * VDIM + 256), BF),
        in_specs=[hbm] * 10,
        out_specs=vmem,
        scratch_shapes=[
            pltpu.SMEM(lengths.shape, jnp.int32),
            pltpu.SMEM(routes.shape, jnp.int32),
            pltpu.SMEM(gate_int.shape, jnp.int32),
            pltpu.VMEM(q_nope.shape, BF),
            pltpu.VMEM(q_rope.shape, BF),
            pltpu.VMEM(residual.shape, BF),
            pltpu.SemaphoreType.DMA((6,)),
            pltpu.VMEM(w_absorb.shape, BF),
            pltpu.VMEM(w_value.shape, BF),
            pltpu.VMEM(cache_latent.shape, BF),
            pltpu.VMEM(cache_rope.shape, BF),
            pltpu.VMEM((width // 128, toks * heads, 128), F32),
            pltpu.VMEM((toks * heads, 2 * ROPE), F32),
            pltpu.VMEM((width // 128, toks * heads, 128), F32),
            pltpu.VMEM((planes, toks, 256), F32),
            pltpu.VMEM((toks * heads // reqs, length), F32),
            pltpu.SemaphoreType.DMA((2,)),
            pltpu.SemaphoreType.DMA((reqs * spans,)),
            pltpu.SemaphoreType.DMA((reqs * spans,)),
        ],
        compiler_params=pltpu.CompilerParams(vmem_limit_bytes=20 * 1024 * 1024),
        name="attention",
    )(*(
        pltpu.with_memory_space_constraint(a, pltpu.HBM)
        for a in (lengths, routes, gate_int, q_nope, q_rope, residual, w_absorb, cache_latent, cache_rope, w_value)
    ))


def half_copies(wg_hbm, wu_hbm, wg, wu, sem, part, stripes):
    experts, depth, _ = wg_hbm.shape
    stripe = depth // stripes
    half = stripe // 2
    groups = []
    for y in range(stripes):
        at = pl.ds(pl.multiple_of(y * stripe + part * half, 16), half)
        to = pl.ds(y * half, half)
        groups.append([
            pltpu.make_async_copy(src.at[e, at, :], dst.at[e, to, :], sem.at[(y * experts + e) * 2 + k])
            for e in range(experts)
            for k, (src, dst) in enumerate(((wg_hbm, wg), (wu_hbm, wu)))
        ])
    return groups


def half_products(blocks_ref, gain_ref, wg, wu, groups, part, acc, swap):
    blocks, rows, _ = blocks_ref.shape
    stripes = len(groups)
    sides = blocks // stripes
    cols = gain_ref.shape[2]
    half = rows // 2
    square = jnp.zeros((rows, cols), F32)
    for y in range(stripes):
        for copy in groups[y]:
            copy.wait()
        for s in range(sides):
            block = blocks_ref[y * sides + s, :, :cols].astype(F32)
            if swap:
                block = jnp.concatenate([block[half:], block[:half]], axis=0)
            square = square + block * block
            scaled = (block * gain_ref[y * 2 + part, pl.ds(s, 1), :]).astype(BF)
            at = pl.ds((y * sides + s) * cols, cols)
            for e in range(len(acc)):
                both = jnp.concatenate([wg[e, at, :], wu[e, at, :]], axis=1)
                acc[e] = acc[e] + jnp.dot(scaled, both, preferred_element_type=F32)
    return acc, jnp.sum(square, axis=-1, keepdims=True)


def pick_rows(blocks_ref, kept_ref, base):
    sides, toks, _ = kept_ref.shape
    at = base + (lax.axis_index("y") * sides + lax.axis_index("side")) * toks
    group = pl.multiple_of(at // 16 * 16, 16)
    for s in range(sides):
        rows = blocks_ref[lax.axis_index("hg") * sides + s, pl.ds(group, 16), :].astype(F32)
        found = rows[:toks]
        for k in range(1, 16 // toks):
            found = jnp.where(at - group == k * toks, rows[k * toks:(k + 1) * toks], found)
        kept_ref[s] = found.astype(BF)


def first_kernel(own_ref, gain_ref, wg_hbm, wu_hbm, acc_ref, sq_ref, kept_ref, wg, wu, sem):
    experts, depth, units = wg_hbm.shape
    rows = own_ref.shape[1]
    core = lax.axis_index("c")
    groups = half_copies(wg_hbm, wu_hbm, wg, wu, sem, core, gain_ref.shape[0] // 2)
    for group in groups:
        for copy in group:
            copy.start()
    acc = [jnp.zeros((rows, 2 * units), F32) for _ in range(experts)]
    acc, square = half_products(own_ref, gain_ref, wg, wu, groups, core, acc, False)
    for e in range(experts):
        acc_ref[e] = acc[e]
    sq_ref[...] = square
    pick_rows(own_ref, kept_ref, 0)


def second_kernel(oth_ref, gain_ref, share_ref, acc_ref, sq_ref, wg_hbm, wu_hbm, wd_hbm, keep_ref, send_ref, kept_ref,
                  wg, wu, wd, sem, sem_down):
    experts, depth, units = wg_hbm.shape
    blocks, rows, _ = oth_ref.shape
    half = rows // 2
    part = 1 - lax.axis_index("c")
    groups = half_copies(wg_hbm, wu_hbm, wg, wu, sem, part, gain_ref.shape[0] // 2)
    downs = [
        pltpu.make_async_copy(wd_hbm.at[e], wd.at[pl.ds(e * units, units), :], sem_down.at[e])
        for e in range(experts)
    ]
    for group in groups:
        for copy in group:
            copy.start()
    for copy in downs:
        copy.start()
    acc, square = half_products(oth_ref, gain_ref, wg, wu, groups, part, [acc_ref[e] for e in range(experts)], True)
    inverse = lax.rsqrt((square + sq_ref[...]) / depth + EPS)
    acts = []
    for e in range(experts):
        both = acc[e] * inverse
        gate, up = both[:, :units], both[:, units:]
        share = share_ref[:, e:e + 1]
        act = gate / (1.0 + jnp.exp(-gate)) * up
        acts.append(jnp.where(share > 0, act * share, 0.0).astype(BF))
    act = jnp.concatenate(acts, axis=1)
    pick_rows(oth_ref, kept_ref, half)
    for copy in downs:
        copy.wait()
    messages, lines, tile = keep_ref.shape
    toks = lines // 2
    for n in range(depth // (2 * tile)):
        left = jnp.dot(act, wd[:, 2 * n * tile:(2 * n + 1) * tile], preferred_element_type=F32)
        right = jnp.dot(act, wd[:, (2 * n + 1) * tile:(2 * n + 2) * tile], preferred_element_type=F32)
        for k in range(blocks):
            for ref, base in ((keep_ref, 0), (send_ref, half)):
                at = slice(base + k * toks, base + (k + 1) * toks)
                ref[n * blocks + k] = jnp.concatenate([left[at], right[at]], axis=0).astype(BF)


def own_half(own, gain, w_gate, w_up, toks):
    experts, depth, units = w_gate.shape
    rows = own.shape[1]
    vmem = pl.BlockSpec(memory_space=pltpu.VMEM)
    hbm = pl.BlockSpec(memory_space=pltpu.HBM)
    w_gate, w_up = (pltpu.with_memory_space_constraint(a, pltpu.HBM) for a in (w_gate, w_up))
    return pl.pallas_call(
        first_kernel,
        out_shape=(
            jax.ShapeDtypeStruct((experts, rows, 2 * units), F32),
            jax.ShapeDtypeStruct((rows, 1), F32),
            jax.ShapeDtypeStruct((gain.shape[1], toks, own.shape[2]), BF),
        ),
        in_specs=[vmem] * 2 + [hbm] * 2,
        out_specs=[vmem] * 3,
        scratch_shapes=[
            pltpu.VMEM((experts, depth // 2, units), BF),
            pltpu.VMEM((experts, depth // 2, units), BF),
            pltpu.SemaphoreType.DMA((gain.shape[0] * experts,)),
        ],
        compiler_params=pltpu.CompilerParams(vmem_limit_bytes=12 * 1024 * 1024),
        cost_estimate=pl.CostEstimate(flops=rows * depth * 512, bytes_accessed=5_000_000, transcendentals=0),
        name="experts_first",
    )(own, gain, w_gate, w_up)


def other_half(oth, gain, share, acc, square, w_gate, w_up, w_down, hgs):
    experts, depth, units = w_gate.shape
    blocks, rows, _ = oth.shape
    shape = jax.ShapeDtypeStruct((hgs * blocks, rows // blocks, depth // hgs // 2), BF)
    vmem = pl.BlockSpec(memory_space=pltpu.VMEM)
    hbm = pl.BlockSpec(memory_space=pltpu.HBM)
    w_gate, w_up, w_down = (pltpu.with_memory_space_constraint(a, pltpu.HBM) for a in (w_gate, w_up, w_down))
    return pl.pallas_call(
        second_kernel,
        out_shape=(shape, shape, jax.ShapeDtypeStruct((gain.shape[1], rows // 2 // blocks, oth.shape[2]), BF)),
        in_specs=[vmem] * 5 + [hbm] * 3,
        out_specs=[vmem] * 3,
        scratch_shapes=[
            pltpu.VMEM((experts, depth // 2, units), BF),
            pltpu.VMEM((experts, depth // 2, units), BF),
            pltpu.VMEM((experts * units, depth), BF),
            pltpu.SemaphoreType.DMA((gain.shape[0] * experts,)),
            pltpu.SemaphoreType.DMA((experts,)),
        ],
        compiler_params=pltpu.CompilerParams(vmem_limit_bytes=18 * 1024 * 1024),
        cost_estimate=pl.CostEstimate(flops=rows * depth * 1024, bytes_accessed=10_000_000, transcendentals=0),
        name="experts_second",
    )(oth, gain, share, acc, square, w_gate, w_up, w_down)


def body(
    q_nope, q_rope, w_absorb, cache_latent, cache_rope, lengths, w_value, w_out, residual, norm_gain,
    routes, gate_int, w_gate, w_up, w_down,
):
    hgs, ys, cores, sides = (lax.axis_size(a) for a in ("hg", "y", "c", "side"))
    hg, y, core, side = (lax.axis_index(a) for a in ("hg", "y", "c", "side"))
    planes = ys * sides
    toks, width = residual.shape
    cols = w_out.shape[1]
    local_experts = w_gate.shape[0]
    experts_all = local_experts * ys * cores

    message = attention(q_nope, q_rope, w_absorb, cache_latent, cache_rope, lengths, w_value, residual, routes, gate_int,
                        planes, sides, experts_all)
    here = lax.all_to_all(message, ("y", "side"), 0, 0, tiled=True)
    there = lax.ppermute(here, "c", SWAP)
    both = jnp.stack([here, there])
    n_val = w_absorb.shape[0] * VDIM
    all_values = both[..., :n_val].reshape(cores * planes * toks, n_val)
    extra = both[..., n_val:]
    window = lax.dynamic_slice_in_dim(extra[..., :3, :], core * 128, 128, 3).reshape(cores * planes, 3 * 128)
    block = (y * cores + core) * sides + side
    mine = lax.dynamic_slice_in_dim(window, lax.rem(block * cols, 128), cols, 1)[:, None]
    gates = extra[..., 3, :toks * experts_all].reshape(cores * planes * toks, experts_all).astype(F32)
    total = jnp.sum(gates, axis=1, keepdims=True)
    first = (y * cores + core) * local_experts
    share = lax.dynamic_slice_in_dim(gates, first, local_experts, 1) * (ROUTE_SCALE / total)

    partial = jnp.dot(all_values, w_out, preferred_element_type=F32).reshape(cores * planes, toks, cols)
    is_row = (jnp.arange(toks) == hg)[None, :, None]
    partial = (partial + jnp.where(is_row, mine.astype(F32), 0.0)).astype(BF).reshape(-1, cols)
    partial = jnp.pad(partial, ((0, 0), (0, -cols % 128)))
    gain = norm_gain.astype(F32).reshape(ys * cores, sides, cols)
    other, share, gain = lax.optimization_barrier((lax.ppermute(partial, "hg", PAIRS_A), share, gain))
    pair = (partial.astype(F32) + other.astype(F32)).astype(BF)
    hidden = (pair.astype(F32) + lax.ppermute(pair, "hg", PAIRS_B).astype(F32)).astype(BF)

    own = lax.all_to_all(jnp.broadcast_to(hidden[None], (planes,) + hidden.shape), ("y", "side"), 0, 0, tiled=True)
    oth = lax.ppermute(own, "c", SWAP)
    acc, square, own_piece = own_half(own, gain, w_gate, w_up, toks)
    keep, send, oth_piece = other_half(oth, gain, share, acc, square, w_gate, w_up, w_down, hgs)
    got = lax.ppermute(send, "c", SWAP)
    quarter = width // hgs
    summed = keep + got
    own_piece, oth_piece = own_piece[..., :cols], oth_piece[..., :cols]
    low = jnp.where(core == 0, own_piece, oth_piece)
    high = jnp.where(core == 0, oth_piece, own_piece)
    kept = jnp.concatenate([low, high], axis=0).transpose(1, 0, 2).reshape(toks, quarter)
    summed, kept = lax.optimization_barrier((summed, kept))
    parts = lax.all_to_all(summed, ("hg", "y", "side"), 0, 0, tiled=True)
    moe = jnp.sum(parts.astype(F32), axis=0)
    moe = jnp.concatenate([moe[:toks], moe[toks:]], axis=1)
    return (kept.astype(F32) + moe).astype(BF)


def solution(mesh):
    devices = mesh.devices
    fine = Mesh(devices.reshape(4, 4, 2, 4), ("hg", "y", "c", "side"))
    grp = ("y", "c")
    plane = ("y", "c", "side")
    in_specs = (
        P(plane, "hg"),
        P(plane, "hg"),
        P("hg", None, None),
        P(plane, None, None),
        P(plane, None, None),
        P(plane),
        P("hg", None, None),
        P("hg", plane),
        P(plane, None),
        P(),
        P(plane, None),
        P(plane, None),
        P(grp, None, ("hg", "side")),
        P(grp, None, ("hg", "side")),
        P(grp, ("hg", "side"), None),
    )
    return jax.shard_map(body, mesh=fine, in_specs=in_specs, out_specs=P(plane, "hg"), check_vma=False)
```

```python
import functools

import jax
import jax.numpy as jnp
from jax import lax
from jax.experimental import pallas as pl
from jax.experimental.pallas import tpu as pltpu
from jax.sharding import Mesh
from jax.sharding import PartitionSpec as P

LAT = 512
ROPE = 64
NOPE = 128
VDIM = 128
QPR = 2
LEN = 4096
EPS = 1e-06
ROUTE_SCALE = 2.5
BF = jnp.bfloat16
F32 = jnp.float32

PAIRS_A = [(0, 1), (1, 0), (2, 3), (3, 2)]
PAIRS_B = [(1, 2), (2, 1), (3, 0), (0, 3)]
SWAP = [(0, 1), (1, 0)]


def attention_kernel(len_hbm, routes_hbm, ints_hbm, qn_hbm, qr_hbm, res_hbm, wa_hbm, lat_hbm, rope_hbm, wv_hbm, out_ref,
                     len_ref, routes_ref, ints_ref, qn_ref, qr_ref, res_ref, sem_in, wa, wv, lat, rope, qs, qps, os, ext, sc, sem_w, sem_l, sem_r, *, span, ahead, sides, experts):
    reqs, length, width = lat_hbm.shape
    heads = wa_hbm.shape[0]
    toks = qn_hbm.shape[0]
    qpr = toks // reqs
    rows = qpr * heads
    spans = length // span
    lanes = width // 128
    scale = (NOPE + ROPE) ** (-0.5)
    absorb = pltpu.make_async_copy(wa_hbm, wa, sem_w.at[0])
    small = [
        pltpu.make_async_copy(a, b, sem_in.at[k])
        for k, (a, b) in enumerate((
            (len_hbm, len_ref), (routes_hbm, routes_ref), (ints_hbm, ints_ref),
            (qn_hbm, qn_ref), (qr_hbm, qr_ref), (res_hbm, res_ref),
        ))
    ]
    for copy in small:
        copy.start()
    absorb.start()
    value = pltpu.make_async_copy(wv_hbm, wv, sem_w.at[1])

    def copies(r, i):
        at = pl.ds(i * span, span)
        return (
            pltpu.make_async_copy(lat_hbm.at[r, at, :], lat.at[r, at, :], sem_l.at[r * spans + i]),
            pltpu.make_async_copy(rope_hbm.at[r, :, at], rope.at[r, :, at], sem_r.at[r * spans + i]),
        )

    chunks = [(r, i) for r in range(reqs) for i in range(spans)]

    def begin(k):
        if k == len(chunks):
            value.start(priority=1)
        elif k < len(chunks):
            r, i = chunks[k]

            def go():
                for copy in copies(r, i):
                    copy.start(priority=1)

            if i == 0:
                go()
            else:
                pl.when(i * span < len_ref[r])(go)

    begin(0)
    for copy in small:
        copy.wait()
    for k in range(1, ahead):
        begin(k)
    planes = out_ref.shape[0]
    cores = 2
    n_val = heads * VDIM
    cols = res_ref.shape[1] // (planes * cores)
    which = lax.broadcasted_iota(jnp.int32, res_ref.shape, 0) == lax.axis_index("hg")
    row = jnp.sum(jnp.where(which, res_ref[...].astype(F32), 0.0), axis=0, keepdims=True)
    lane = lax.broadcasted_iota(jnp.int32, (1, 128), 1)
    dense = jnp.zeros((1, 128), jnp.int32)
    for j in range(toks):
        for k in range(routes_ref.shape[1]):
            dense = dense + jnp.where(lane == j * experts + routes_ref[j, k], ints_ref[j, k], 0)
    dense = dense.astype(F32)
    for p in range(planes):
        y, side = divmod(p, sides)
        for c in range(cores):
            start = ((y * cores + c) * sides + side) * cols // 128
            for t in range(3):
                tile = min(start + t, res_ref.shape[1] // 128 - 1)
                ext[p, pl.ds(t, 1), c * 128:(c + 1) * 128] = row[:, tile * 128:(tile + 1) * 128]
        ext[p, pl.ds(3, 1), :] = jnp.concatenate([dense, dense], axis=1)
    for p in range(planes):
        out_ref[p, :, n_val:] = ext[p].astype(BF)
    turned = qr_ref[...].astype(F32)
    for h in range(heads):
        pair = turned[:, (h // 2) * 2 * ROPE:(h // 2 + 1) * 2 * ROPE]
        if h % 2:
            pair = jnp.concatenate([pair[:, ROPE:], pair[:, :ROPE]], axis=1)
        qps[pl.ds(h, toks, stride=heads), :] = pair
    absorb.wait()
    for h in range(heads):
        latent = jnp.dot(qn_ref[:, h * NOPE:(h + 1) * NOPE], wa[h], preferred_element_type=F32)
        for c in range(lanes):
            qs[c, pl.ds(h, toks, stride=heads), :] = latent[:, c * 128:(c + 1) * 128]
    def scores(r, count):
        at = pl.ds(r * rows, rows)
        query = jnp.concatenate([qs[c, at, :] for c in range(lanes)], axis=1).astype(BF)
        rotary = qps[at, :ROPE].astype(BF)
        limit = len_ref[r] - qpr + lax.broadcasted_iota(jnp.int32, (rows, 1), 0) // heads
        out = []
        for i in range(count):
            to = pl.ds(i * span, span)
            for copy in copies(r, i):
                copy.wait()
            s = lax.dot_general(query, lat[r, to, :], (((1,), (1,)), ((), ())), preferred_element_type=F32)
            s = (s + jnp.dot(rotary, rope[r, :, to], preferred_element_type=F32)) * scale
            position = i * span + lax.broadcasted_iota(jnp.int32, (rows, span), 1)
            out.append(jnp.where(position <= limit, s, -jnp.inf))
        return out

    def mix(r, s):
        top = functools.reduce(jnp.maximum, [jnp.max(x, axis=1, keepdims=True) for x in s])
        p = [jnp.exp(x - top) for x in s]
        norm = sum(jnp.sum(x, axis=1, keepdims=True) for x in p)
        acc = sum(
            jnp.dot(x.astype(BF), lat[r, pl.ds(i * span, span), :], preferred_element_type=F32)
            for i, x in enumerate(p)
        )
        result = acc / norm
        for c in range(lanes):
            os[c, pl.ds(r * rows, rows), :] = result[:, c * 128:(c + 1) * 128]

    def attend(first, second):
        one = scores(0, first)
        two = scores(1, second)
        mix(0, one)
        mix(1, two)

    counts = [(len_ref[r] + span - 1) // span for r in range(reqs)]
    for first in range(1, spans + 1):
        for second in range(1, spans + 1):
            pl.when((counts[0] == first) & (counts[1] == second))(functools.partial(attend, first, second))
    value.wait()
    for h in range(heads):
        at = pl.ds(h, toks, stride=heads)
        o = jnp.concatenate([os[c, at, :] for c in range(lanes)], axis=1).astype(BF)
        head = jnp.dot(o, wv[h], preferred_element_type=F32).astype(BF)
        for k in range(planes):
            out_ref[k, :, h * VDIM:(h + 1) * VDIM] = head


def attention(q_nope, q_rope, w_absorb, cache_latent, cache_rope, lengths, w_value, residual, routes, gate_int,
              planes, sides, experts, span=2048, ahead=5):
    reqs, length, width = cache_latent.shape
    spans = length // span
    heads = w_absorb.shape[0]
    toks = q_nope.shape[0]
    hbm = pl.BlockSpec(memory_space=pltpu.HBM)
    vmem = pl.BlockSpec(memory_space=pltpu.VMEM)
    return pl.pallas_call(
        functools.partial(attention_kernel, span=span, ahead=ahead, sides=sides, experts=experts),
        out_shape=pltpu.VMEM((planes, toks, heads * VDIM + 256), BF),
        in_specs=[hbm] * 10,
        out_specs=vmem,
        scratch_shapes=[
            pltpu.SMEM(lengths.shape, jnp.int32),
            pltpu.SMEM(routes.shape, jnp.int32),
            pltpu.SMEM(gate_int.shape, jnp.int32),
            pltpu.VMEM(q_nope.shape, BF),
            pltpu.VMEM(q_rope.shape, BF),
            pltpu.VMEM(residual.shape, BF),
            pltpu.SemaphoreType.DMA((6,)),
            pltpu.VMEM(w_absorb.shape, BF),
            pltpu.VMEM(w_value.shape, BF),
            pltpu.VMEM(cache_latent.shape, BF),
            pltpu.VMEM(cache_rope.shape, BF),
            pltpu.VMEM((width // 128, toks * heads, 128), F32),
            pltpu.VMEM((toks * heads, 2 * ROPE), F32),
            pltpu.VMEM((width // 128, toks * heads, 128), F32),
            pltpu.VMEM((planes, toks, 256), F32),
            pltpu.VMEM((reqs, toks * heads // reqs, length), F32),
            pltpu.SemaphoreType.DMA((2,)),
            pltpu.SemaphoreType.DMA((reqs * spans,)),
            pltpu.SemaphoreType.DMA((reqs * spans,)),
        ],
        compiler_params=pltpu.CompilerParams(vmem_limit_bytes=20 * 1024 * 1024),
        name="attention",
    )(*(
        pltpu.with_memory_space_constraint(a, pltpu.HBM)
        for a in (lengths, routes, gate_int, q_nope, q_rope, residual, w_absorb, cache_latent, cache_rope, w_value)
    ))


def half_copies(wg_hbm, wu_hbm, wg, wu, sem, part, stripes):
    experts, depth, _ = wg_hbm.shape
    stripe = depth // stripes
    half = stripe // 2
    groups = []
    for y in range(stripes):
        at = pl.ds(pl.multiple_of(y * stripe + part * half, 16), half)
        to = pl.ds(y * half, half)
        groups.append([
            pltpu.make_async_copy(src.at[e, at, :], dst.at[e, to, :], sem.at[(y * experts + e) * 2 + k])
            for e in range(experts)
            for k, (src, dst) in enumerate(((wg_hbm, wg), (wu_hbm, wu)))
        ])
    return groups


def half_products(blocks_ref, gain_ref, wg, wu, groups, part, acc, swap):
    blocks, rows, _ = blocks_ref.shape
    stripes = len(groups)
    sides = blocks // stripes
    cols = gain_ref.shape[2]
    half = rows // 2
    square = jnp.zeros((rows, cols), F32)
    for y in range(stripes):
        for copy in groups[y]:
            copy.wait()
        for s in range(sides):
            block = blocks_ref[y * sides + s, :, :cols].astype(F32)
            if swap:
                block = jnp.concatenate([block[half:], block[:half]], axis=0)
            square = square + block * block
            scaled = (block * gain_ref[y * 2 + part, pl.ds(s, 1), :]).astype(BF)
            at = pl.ds((y * sides + s) * cols, cols)
            for e in range(len(acc)):
                both = jnp.concatenate([wg[e, at, :], wu[e, at, :]], axis=1)
                acc[e] = acc[e] + jnp.dot(scaled, both, preferred_element_type=F32)
    return acc, jnp.sum(square, axis=-1, keepdims=True)


def pick_rows(blocks_ref, kept_ref, base):
    sides, toks, _ = kept_ref.shape
    at = base + (lax.axis_index("y") * sides + lax.axis_index("side")) * toks
    group = pl.multiple_of(at // 16 * 16, 16)
    for s in range(sides):
        rows = blocks_ref[lax.axis_index("hg") * sides + s, pl.ds(group, 16), :].astype(F32)
        found = rows[:toks]
        for k in range(1, 16 // toks):
            found = jnp.where(at - group == k * toks, rows[k * toks:(k + 1) * toks], found)
        kept_ref[s] = found.astype(BF)


def first_kernel(own_ref, gain_ref, wg_hbm, wu_hbm, acc_ref, sq_ref, kept_ref, wg, wu, sem):
    experts, depth, units = wg_hbm.shape
    rows = own_ref.shape[1]
    core = lax.axis_index("c")
    groups = half_copies(wg_hbm, wu_hbm, wg, wu, sem, core, gain_ref.shape[0] // 2)
    for group in groups:
        for copy in group:
            copy.start()
    acc = [jnp.zeros((rows, 2 * units), F32) for _ in range(experts)]
    acc, square = half_products(own_ref, gain_ref, wg, wu, groups, core, acc, False)
    for e in range(experts):
        acc_ref[e] = acc[e]
    sq_ref[...] = square
    pick_rows(own_ref, kept_ref, 0)


def second_kernel(oth_ref, gain_ref, share_ref, acc_ref, sq_ref, wg_hbm, wu_hbm, wd_hbm, keep_ref, low_ref, high_ref, kept_ref,
                  wg, wu, wd, sem, sem_down):
    experts, depth, units = wg_hbm.shape
    blocks, rows, _ = oth_ref.shape
    half = rows // 2
    part = 1 - lax.axis_index("c")
    groups = half_copies(wg_hbm, wu_hbm, wg, wu, sem, part, gain_ref.shape[0] // 2)
    downs = [
        pltpu.make_async_copy(wd_hbm.at[e], wd.at[pl.ds(e * units, units), :], sem_down.at[e])
        for e in range(experts)
    ]
    for group in groups:
        for copy in group:
            copy.start()
    for copy in downs:
        copy.start(priority=1)
    acc, square = half_products(oth_ref, gain_ref, wg, wu, groups, part, [acc_ref[e] for e in range(experts)], True)
    inverse = lax.rsqrt((square + sq_ref[...]) / depth + EPS)
    acts = []
    for e in range(experts):
        both = acc[e] * inverse
        gate, up = both[:, :units], both[:, units:]
        share = share_ref[:, e:e + 1]
        act = gate / (1.0 + jnp.exp(-gate)) * up
        acts.append(jnp.where(share > 0, act * share, 0.0).astype(BF))
    act = jnp.concatenate(acts, axis=1)
    pick_rows(oth_ref, kept_ref, half)
    for copy in downs:
        copy.wait()
    messages, lines, tile = keep_ref.shape
    toks = lines // 2
    for n in range(depth // (2 * tile)):
        left = jnp.dot(act, wd[:, 2 * n * tile:(2 * n + 1) * tile], preferred_element_type=F32)
        right = jnp.dot(act, wd[:, (2 * n + 1) * tile:(2 * n + 2) * tile], preferred_element_type=F32)
        for k in range(blocks):
            at = slice(k * toks, (k + 1) * toks)
            keep_ref[n * blocks + k] = jnp.concatenate([left[at], right[at]], axis=0).astype(BF)
            at = slice(half + k * toks, half + (k + 1) * toks)
            send_ref, place = (low_ref, n) if n * blocks < low_ref.shape[0] else (high_ref, n - low_ref.shape[0] // blocks)
            send_ref[place * blocks + k] = jnp.concatenate([left[at], right[at]], axis=0).astype(BF)


def own_half(own, gain, w_gate, w_up, toks):
    experts, depth, units = w_gate.shape
    rows = own.shape[1]
    vmem = pl.BlockSpec(memory_space=pltpu.VMEM)
    hbm = pl.BlockSpec(memory_space=pltpu.HBM)
    w_gate, w_up = (pltpu.with_memory_space_constraint(a, pltpu.HBM) for a in (w_gate, w_up))
    return pl.pallas_call(
        first_kernel,
        out_shape=(
            jax.ShapeDtypeStruct((experts, rows, 2 * units), F32),
            jax.ShapeDtypeStruct((rows, 1), F32),
            jax.ShapeDtypeStruct((gain.shape[1], toks, own.shape[2]), BF),
        ),
        in_specs=[vmem] * 2 + [hbm] * 2,
        out_specs=[vmem] * 3,
        scratch_shapes=[
            pltpu.VMEM((experts, depth // 2, units), BF),
            pltpu.VMEM((experts, depth // 2, units), BF),
            pltpu.SemaphoreType.DMA((gain.shape[0] * experts,)),
        ],
        compiler_params=pltpu.CompilerParams(vmem_limit_bytes=12 * 1024 * 1024),
        cost_estimate=pl.CostEstimate(flops=rows * depth * 512, bytes_accessed=5_000_000, transcendentals=0),
        name="experts_first",
    )(own, gain, w_gate, w_up)


def other_half(oth, gain, share, acc, square, w_gate, w_up, w_down, hgs):
    experts, depth, units = w_gate.shape
    blocks, rows, _ = oth.shape
    shape = jax.ShapeDtypeStruct((hgs * blocks, rows // blocks, depth // hgs // 2), BF)
    part = jax.ShapeDtypeStruct((hgs * blocks // 2,) + shape.shape[1:], BF)
    vmem = pl.BlockSpec(memory_space=pltpu.VMEM)
    hbm = pl.BlockSpec(memory_space=pltpu.HBM)
    w_gate, w_up, w_down = (pltpu.with_memory_space_constraint(a, pltpu.HBM) for a in (w_gate, w_up, w_down))
    return pl.pallas_call(
        second_kernel,
        out_shape=(shape, part, part, jax.ShapeDtypeStruct((gain.shape[1], rows // 2 // blocks, oth.shape[2]), BF)),
        in_specs=[vmem] * 5 + [hbm] * 3,
        out_specs=[vmem] * 4,
        scratch_shapes=[
            pltpu.VMEM((experts, depth // 2, units), BF),
            pltpu.VMEM((experts, depth // 2, units), BF),
            pltpu.VMEM((experts * units, depth), BF),
            pltpu.SemaphoreType.DMA((gain.shape[0] * experts,)),
            pltpu.SemaphoreType.DMA((experts,)),
        ],
        compiler_params=pltpu.CompilerParams(vmem_limit_bytes=18 * 1024 * 1024),
        cost_estimate=pl.CostEstimate(flops=rows * depth * 1024, bytes_accessed=10_000_000, transcendentals=0),
        name="experts_second",
    )(oth, gain, share, acc, square, w_gate, w_up, w_down)


def body(
    q_nope, q_rope, w_absorb, cache_latent, cache_rope, lengths, w_value, w_out, residual, norm_gain,
    routes, gate_int, w_gate, w_up, w_down,
):
    hgs, ys, cores, sides = (lax.axis_size(a) for a in ("hg", "y", "c", "side"))
    hg, y, core, side = (lax.axis_index(a) for a in ("hg", "y", "c", "side"))
    planes = ys * sides
    toks, width = residual.shape
    cols = w_out.shape[1]
    local_experts = w_gate.shape[0]
    experts_all = local_experts * ys * cores

    message = attention(q_nope, q_rope, w_absorb, cache_latent, cache_rope, lengths, w_value, residual, routes, gate_int,
                        planes, sides, experts_all)
    here = lax.all_to_all(message, ("y", "side"), 0, 0, tiled=True)
    there = lax.ppermute(here, "c", SWAP)
    both = jnp.stack([here, there])
    n_val = w_absorb.shape[0] * VDIM
    all_values = both[..., :n_val].reshape(cores * planes * toks, n_val)
    extra = both[..., n_val:]
    window = lax.dynamic_slice_in_dim(extra[..., :3, :], core * 128, 128, 3).reshape(cores * planes, 3 * 128)
    block = (y * cores + core) * sides + side
    mine = lax.dynamic_slice_in_dim(window, lax.rem(block * cols, 128), cols, 1)[:, None]
    gates = extra[..., 3, :toks * experts_all].reshape(cores * planes * toks, experts_all).astype(F32)
    total = jnp.sum(gates, axis=1, keepdims=True)
    first = (y * cores + core) * local_experts
    share = lax.dynamic_slice_in_dim(gates, first, local_experts, 1) * (ROUTE_SCALE / total)

    partial = jnp.dot(all_values, w_out, preferred_element_type=F32).reshape(cores * planes, toks, cols)
    is_row = (jnp.arange(toks) == hg)[None, :, None]
    partial = (partial + jnp.where(is_row, mine.astype(F32), 0.0)).astype(BF).reshape(-1, cols)
    partial = jnp.pad(partial, ((0, 0), (0, -cols % 128)))
    gain = norm_gain.astype(F32).reshape(ys * cores, sides, cols)
    other, share, gain = lax.optimization_barrier((lax.ppermute(partial, "hg", PAIRS_A), share, gain))
    pair = (partial.astype(F32) + other.astype(F32)).astype(BF)
    hidden = (pair.astype(F32) + lax.ppermute(pair, "hg", PAIRS_B).astype(F32)).astype(BF)

    own = lax.all_to_all(jnp.broadcast_to(hidden[None], (planes,) + hidden.shape), ("y", "side"), 0, 0, tiled=True)
    oth = lax.ppermute(own, "c", SWAP)
    acc, square, own_piece = own_half(own, gain, w_gate, w_up, toks)
    keep, low, high, oth_piece = other_half(oth, gain, share, acc, square, w_gate, w_up, w_down, hgs)
    got = jnp.concatenate([lax.ppermute(low, "c", SWAP), lax.ppermute(high, "c", SWAP)], axis=0)
    quarter = width // hgs
    summed = keep + got
    own_piece, oth_piece = own_piece[..., :cols], oth_piece[..., :cols]
    kept = jnp.where(core == 0, jnp.concatenate([own_piece, oth_piece]), jnp.concatenate([oth_piece, own_piece]))
    kept = kept.transpose(1, 0, 2).reshape(toks, quarter)
    summed, kept = lax.optimization_barrier((summed, kept))
    parts = lax.all_to_all(summed, ("hg", "y", "side"), 0, 0, tiled=True)
    moe = jnp.sum(parts.astype(F32), axis=0)
    moe = jnp.concatenate([moe[:toks], moe[toks:]], axis=1)
    return (kept.astype(F32) + moe).astype(BF)


def solution(mesh):
    devices = mesh.devices
    fine = Mesh(devices.reshape(4, 4, 2, 4), ("hg", "y", "c", "side"))
    grp = ("y", "c")
    plane = ("y", "c", "side")
    in_specs = (
        P(plane, "hg"),
        P(plane, "hg"),
        P("hg", None, None),
        P(plane, None, None),
        P(plane, None, None),
        P(plane),
        P("hg", None, None),
        P("hg", plane),
        P(plane, None),
        P(),
        P(plane, None),
        P(plane, None),
        P(grp, None, ("hg", "side")),
        P(grp, None, ("hg", "side")),
        P(grp, ("hg", "side"), None),
    )
    return jax.shard_map(body, mesh=fine, in_specs=in_specs, out_specs=P(plane, "hg"), check_vma=False)
```

```python
import functools

import jax
import jax.numpy as jnp
from jax import lax
from jax.experimental import pallas as pl
from jax.experimental.pallas import tpu as pltpu
from jax.sharding import Mesh
from jax.sharding import PartitionSpec as P

LAT = 512
ROPE = 64
NOPE = 128
VDIM = 128
QPR = 2
LEN = 4096
EPS = 1e-06
ROUTE_SCALE = 2.5
BF = jnp.bfloat16
F32 = jnp.float32

PAIRS_A = [(0, 1), (1, 0), (2, 3), (3, 2)]
PAIRS_B = [(1, 2), (2, 1), (3, 0), (0, 3)]
SWAP = [(0, 1), (1, 0)]


def attention_kernel(len_hbm, routes_hbm, ints_hbm, qn_hbm, qr_hbm, res_hbm, wa_hbm, lat_hbm, rope_hbm, wv_hbm, out_ref,
                     len_ref, routes_ref, ints_ref, qn_ref, qr_ref, res_ref, sem_in, wa, wv, lat, rope, qs, qps, os, ext, sc, sem_w, sem_l, sem_r, *, span, ahead, sides, experts):
    reqs, length, width = lat_hbm.shape
    heads = wa_hbm.shape[0]
    toks = qn_hbm.shape[0]
    qpr = toks // reqs
    rows = qpr * heads
    spans = length // span
    lanes = width // 128
    scale = (NOPE + ROPE) ** (-0.5)
    absorb = pltpu.make_async_copy(wa_hbm, wa, sem_w.at[0])
    small = [
        pltpu.make_async_copy(a, b, sem_in.at[k])
        for k, (a, b) in enumerate((
            (len_hbm, len_ref), (routes_hbm, routes_ref), (ints_hbm, ints_ref),
            (qn_hbm, qn_ref), (qr_hbm, qr_ref), (res_hbm, res_ref),
        ))
    ]
    for copy in small:
        copy.start()
    absorb.start()
    value = pltpu.make_async_copy(wv_hbm, wv, sem_w.at[1])

    def copies(r, i):
        at = pl.ds(i * span, span)
        return (
            pltpu.make_async_copy(lat_hbm.at[r, at, :], lat.at[r, at, :], sem_l.at[r * spans + i]),
            pltpu.make_async_copy(rope_hbm.at[r, :, at], rope.at[r, :, at], sem_r.at[r * spans + i]),
        )

    chunks = [(r, i) for r in range(reqs) for i in range(spans)]

    def begin(k):
        if k == len(chunks):
            value.start(priority=1)
        elif k < len(chunks):
            r, i = chunks[k]

            def go():
                for copy in copies(r, i):
                    copy.start(priority=1)

            if i == 0:
                go()
            else:
                pl.when(i * span < len_ref[r])(go)

    begin(0)
    for copy in small:
        copy.wait()
    for k in range(1, ahead):
        begin(k)
    planes = out_ref.shape[0]
    cores = 2
    n_val = heads * VDIM
    cols = res_ref.shape[1] // (planes * cores)
    which = lax.broadcasted_iota(jnp.int32, res_ref.shape, 0) == lax.axis_index("hg")
    row = jnp.sum(jnp.where(which, res_ref[...].astype(F32), 0.0), axis=0, keepdims=True)
    lane = lax.broadcasted_iota(jnp.int32, (1, 128), 1)
    dense = jnp.zeros((1, 128), jnp.int32)
    for j in range(toks):
        for k in range(routes_ref.shape[1]):
            dense = dense + jnp.where(lane == j * experts + routes_ref[j, k], ints_ref[j, k], 0)
    dense = dense.astype(F32)
    for p in range(planes):
        y, side = divmod(p, sides)
        for c in range(cores):
            start = ((y * cores + c) * sides + side) * cols // 128
            for t in range(3):
                tile = min(start + t, res_ref.shape[1] // 128 - 1)
                ext[p, pl.ds(t, 1), c * 128:(c + 1) * 128] = row[:, tile * 128:(tile + 1) * 128]
        ext[p, pl.ds(3, 1), :] = jnp.concatenate([dense, dense], axis=1)
    for p in range(planes):
        out_ref[p, :, n_val:] = ext[p].astype(BF)
    turned = qr_ref[...].astype(F32)
    for h in range(heads):
        pair = turned[:, (h // 2) * 2 * ROPE:(h // 2 + 1) * 2 * ROPE]
        if h % 2:
            pair = jnp.concatenate([pair[:, ROPE:], pair[:, :ROPE]], axis=1)
        qps[pl.ds(h, toks, stride=heads), :] = pair
    absorb.wait()
    for h in range(heads):
        latent = jnp.dot(qn_ref[:, h * NOPE:(h + 1) * NOPE], wa[h], preferred_element_type=F32)
        for c in range(lanes):
            qs[c, pl.ds(h, toks, stride=heads), :] = latent[:, c * 128:(c + 1) * 128]
    def scores(r, count):
        at = pl.ds(r * rows, rows)
        query = jnp.concatenate([qs[c, at, :] for c in range(lanes)], axis=1).astype(BF)
        rotary = qps[at, :ROPE].astype(BF)
        limit = len_ref[r] - qpr + lax.broadcasted_iota(jnp.int32, (rows, 1), 0) // heads
        out = []
        for i in range(count):
            to = pl.ds(i * span, span)
            for copy in copies(r, i):
                copy.wait()
            s = lax.dot_general(query, lat[r, to, :], (((1,), (1,)), ((), ())), preferred_element_type=F32)
            s = (s + jnp.dot(rotary, rope[r, :, to], preferred_element_type=F32)) * scale
            position = i * span + lax.broadcasted_iota(jnp.int32, (rows, span), 1)
            out.append(jnp.where(position <= limit, s, -jnp.inf))
        return out

    def mix(r, s):
        top = functools.reduce(jnp.maximum, [jnp.max(x, axis=1, keepdims=True) for x in s])
        p = [jnp.exp(x - top) for x in s]
        norm = sum(jnp.sum(x, axis=1, keepdims=True) for x in p)
        acc = sum(
            jnp.dot(x.astype(BF), lat[r, pl.ds(i * span, span), :], preferred_element_type=F32)
            for i, x in enumerate(p)
        )
        result = acc / norm
        for c in range(lanes):
            os[c, pl.ds(r * rows, rows), :] = result[:, c * 128:(c + 1) * 128]

    def attend(first, second):
        one = scores(0, first)
        two = scores(1, second)
        mix(0, one)
        mix(1, two)

    counts = [(len_ref[r] + span - 1) // span for r in range(reqs)]
    for first in range(1, spans + 1):
        for second in range(1, spans + 1):
            pl.when((counts[0] == first) & (counts[1] == second))(functools.partial(attend, first, second))
    value.wait()
    for h in range(heads):
        at = pl.ds(h, toks, stride=heads)
        o = jnp.concatenate([os[c, at, :] for c in range(lanes)], axis=1).astype(BF)
        head = jnp.dot(o, wv[h], preferred_element_type=F32).astype(BF)
        for k in range(planes):
            out_ref[k, :, h * VDIM:(h + 1) * VDIM] = head


def attention(q_nope, q_rope, w_absorb, cache_latent, cache_rope, lengths, w_value, residual, routes, gate_int,
              planes, sides, experts, span=2048, ahead=5):
    reqs, length, width = cache_latent.shape
    spans = length // span
    heads = w_absorb.shape[0]
    toks = q_nope.shape[0]
    hbm = pl.BlockSpec(memory_space=pltpu.HBM)
    vmem = pl.BlockSpec(memory_space=pltpu.VMEM)
    return pl.pallas_call(
        functools.partial(attention_kernel, span=span, ahead=ahead, sides=sides, experts=experts),
        out_shape=pltpu.VMEM((planes, toks, heads * VDIM + 256), BF),
        in_specs=[hbm] * 10,
        out_specs=vmem,
        scratch_shapes=[
            pltpu.SMEM(lengths.shape, jnp.int32),
            pltpu.SMEM(routes.shape, jnp.int32),
            pltpu.SMEM(gate_int.shape, jnp.int32),
            pltpu.VMEM(q_nope.shape, BF),
            pltpu.VMEM(q_rope.shape, BF),
            pltpu.VMEM(residual.shape, BF),
            pltpu.SemaphoreType.DMA((6,)),
            pltpu.VMEM(w_absorb.shape, BF),
            pltpu.VMEM(w_value.shape, BF),
            pltpu.VMEM(cache_latent.shape, BF),
            pltpu.VMEM(cache_rope.shape, BF),
            pltpu.VMEM((width // 128, toks * heads, 128), F32),
            pltpu.VMEM((toks * heads, 2 * ROPE), F32),
            pltpu.VMEM((width // 128, toks * heads, 128), F32),
            pltpu.VMEM((planes, toks, 256), F32),
            pltpu.VMEM((reqs, toks * heads // reqs, length), F32),
            pltpu.SemaphoreType.DMA((2,)),
            pltpu.SemaphoreType.DMA((reqs * spans,)),
            pltpu.SemaphoreType.DMA((reqs * spans,)),
        ],
        compiler_params=pltpu.CompilerParams(vmem_limit_bytes=20 * 1024 * 1024),
        name="attention",
    )(*(
        pltpu.with_memory_space_constraint(a, pltpu.HBM)
        for a in (lengths, routes, gate_int, q_nope, q_rope, residual, w_absorb, cache_latent, cache_rope, w_value)
    ))


def experts_kernel(rows_ref, gain_ref, share_ref, wg0, wu0, wd0, wg1, wu1, wd1, out_ref, kept_ref,
                   wg, wu, wd, sem, sem_down, *, ahead):
    local, depth, units = wg0.shape
    experts = 2 * local
    blocks, rows, lanes = rows_ref.shape
    sides, cols = gain_ref.shape[1:]
    stripes = blocks // sides
    stripe = depth // stripes
    core = lax.axis_index("c")
    groups = []
    for y in range(stripes):
        at = pl.ds(y * stripe, stripe)
        groups.append([
            pltpu.make_async_copy(src.at[:, at, :], dst.at[pl.ds(k * local, local), at, :], sem.at[y * 4 + 2 * k + j])
            for k in range(2)
            for j, (src, dst) in enumerate((((wg0, wg1)[k], wg), ((wu0, wu1)[k], wu)))
        ])
    messages, lines, tile = out_ref.shape
    toks = lines // 2
    parts = depth // (2 * tile)
    downs = []
    for n in range(parts):
        at = pl.ds(2 * n * tile, 2 * tile)
        downs.append([
            pltpu.make_async_copy(src.at[:, :, at], wd.at[pl.ds(k * local, local), :, at], sem_down.at[n * 2 + k])
            for k, src in enumerate((wd0, wd1))
        ])
    queue = groups + downs
    for y in range(ahead):
        for copy in groups[y]:
            copy.start()
    pick_rows(rows_ref, kept_ref)
    acc = [jnp.zeros((rows, 2 * units), F32) for _ in range(experts)]
    square = jnp.zeros((rows, cols), F32)
    for y in range(stripes):
        for copy in queue[y + ahead]:
            copy.start()
        for copy in groups[y]:
            copy.wait()
        for s in range(sides):
            for other in range(2):
                part = core if other == 0 else 1 - core
                first = other * (lanes // 2)
                block = rows_ref[y * sides + s, :, first:first + cols].astype(F32)
                square = square + block * block
                scaled = (block * gain_ref[y * 2 + part, pl.ds(s, 1), :]).astype(BF)
                at = pl.ds(pl.multiple_of(y * stripe + part * (stripe // 2) + s * cols, 16), cols)
                for e in range(experts):
                    both = jnp.concatenate([wg[e, at, :], wu[e, at, :]], axis=1)
                    acc[e] = acc[e] + jnp.dot(scaled, both, preferred_element_type=F32)
    inverse = lax.rsqrt(jnp.sum(square, axis=-1, keepdims=True) / depth + EPS)
    acts = []
    for e in range(experts):
        both = acc[e] * inverse
        gate, up = both[:, :units], both[:, units:]
        share = share_ref[:, e:e + 1]
        act = gate / (1.0 + jnp.exp(-gate)) * up
        acts.append(jnp.where(share > 0, act * share, 0.0).astype(BF))
    act = jnp.concatenate(acts, axis=1)
    for n in range(parts):
        if stripes + n + ahead < len(queue):
            for copy in queue[stripes + n + ahead]:
                copy.start()
        for copy in downs[n]:
            copy.wait()
        down = wd[:, :, 2 * n * tile:(2 * n + 2) * tile].reshape(experts * units, 2 * tile)
        left = jnp.dot(act, down[:, :tile], preferred_element_type=F32)
        right = jnp.dot(act, down[:, tile:], preferred_element_type=F32)
        for k in range(blocks):
            at = slice(k * toks, (k + 1) * toks)
            out_ref[n * blocks + k] = jnp.concatenate([left[at], right[at]], axis=0).astype(BF)


def pick_rows(blocks_ref, kept_ref):
    sides, toks, _ = kept_ref.shape
    at = (lax.axis_index("y") * sides + lax.axis_index("side")) * toks
    group = pl.multiple_of(at // 16 * 16, 16)
    for s in range(sides):
        rows = blocks_ref[lax.axis_index("hg") * sides + s, pl.ds(group, 16), :].astype(F32)
        found = rows[:toks]
        for k in range(1, 16 // toks):
            found = jnp.where(at - group == k * toks, rows[k * toks:(k + 1) * toks], found)
        kept_ref[s] = found.astype(BF)


def run_experts(rows, gain, share, own, other, hgs, ahead=3):
    local, depth, units = own[0].shape
    experts = 2 * local
    blocks, count, lanes = rows.shape
    toks = count // blocks
    vmem = pl.BlockSpec(memory_space=pltpu.VMEM)
    hbm = pl.BlockSpec(memory_space=pltpu.HBM)
    weights = [pltpu.with_memory_space_constraint(a, pltpu.HBM) for a in (*own, *other)]
    return pl.pallas_call(
        functools.partial(experts_kernel, ahead=ahead),
        out_shape=(
            pltpu.VMEM((hgs * blocks, 2 * toks, depth // hgs // 2), BF),
            jax.ShapeDtypeStruct((gain.shape[1], toks, lanes), BF),
        ),
        in_specs=[vmem] * 3 + [hbm] * 6,
        out_specs=[vmem] * 2,
        scratch_shapes=[
            pltpu.VMEM((experts, depth, units), BF),
            pltpu.VMEM((experts, depth, units), BF),
            pltpu.VMEM((experts, units, depth), BF),
            pltpu.SemaphoreType.DMA((blocks // gain.shape[1] * 4,)),
            pltpu.SemaphoreType.DMA((hgs * 2,)),
        ],
        compiler_params=pltpu.CompilerParams(vmem_limit_bytes=32 * 1024 * 1024),
        cost_estimate=pl.CostEstimate(flops=count * depth * 3072, bytes_accessed=24_000_000, transcendentals=0),
        name="experts",
    )(rows, gain, share, *weights)


def body(
    q_nope, q_rope, w_absorb, cache_latent, cache_rope, lengths, w_value, w_out, residual, norm_gain,
    routes, gate_int, w_gate, w_up, w_down,
):
    hgs, ys, cores, sides = (lax.axis_size(a) for a in ("hg", "y", "c", "side"))
    hg, y, core, side = (lax.axis_index(a) for a in ("hg", "y", "c", "side"))
    planes = ys * sides
    toks, width = residual.shape
    cols = w_out.shape[1]
    local_experts = w_gate.shape[0]
    experts_all = local_experts * ys * cores

    message = attention(q_nope, q_rope, w_absorb, cache_latent, cache_rope, lengths, w_value, residual, routes, gate_int,
                        planes, sides, experts_all)
    message, w_out_, norm_gain = lax.optimization_barrier((message, w_out, norm_gain))
    out_there = lax.ppermute(w_out_, "c", SWAP)
    gain = norm_gain.astype(F32).reshape(ys * cores, sides, cols)
    gain, w_gate_, w_up_, w_down_ = lax.optimization_barrier((gain, w_gate, w_up, w_down))
    other = tuple(lax.ppermute(w, "c", SWAP) for w in (w_gate_, w_up_, w_down_))
    here = lax.all_to_all(message, ("y", "side"), 0, 0, tiled=True)
    n_val = w_absorb.shape[0] * VDIM
    values = here[..., :n_val].reshape(planes * toks, n_val)
    extra = here[..., n_val:]
    is_row = (jnp.arange(toks) == hg)[None, :, None]
    halves = []
    for part, weights in ((core, w_out), (1 - core, out_there)):
        window = lax.dynamic_slice_in_dim(extra[:, :3], part * 128, 128, 2).reshape(planes, 3 * 128)
        block = (y * cores + part) * sides + side
        mine = lax.dynamic_slice_in_dim(window, lax.rem(block * cols, 128), cols, 1)[:, None]
        half = jnp.dot(values, weights, preferred_element_type=F32).reshape(planes, toks, cols)
        half = (half + jnp.where(is_row, mine.astype(F32), 0.0)).astype(BF).reshape(planes * toks, cols)
        halves.append(jnp.pad(half, ((0, 0), (0, -cols % 128))))
    partial = jnp.concatenate(halves, axis=1)
    gates = extra[:, 3, :toks * experts_all].reshape(planes * toks, experts_all).astype(F32)
    total = jnp.sum(gates, axis=1, keepdims=True)
    share = jnp.concatenate(
        [
            lax.dynamic_slice_in_dim(gates, (y * cores + part) * local_experts, local_experts, 1)
            for part in (core, 1 - core)
        ],
        axis=1,
    ) * (ROUTE_SCALE / total)
    got, share = lax.optimization_barrier((lax.ppermute(partial, "hg", PAIRS_A), share))
    pair = (partial.astype(F32) + got.astype(F32)).astype(BF)
    hidden = (pair.astype(F32) + lax.ppermute(pair, "hg", PAIRS_B).astype(F32)).astype(BF)

    rows = lax.all_to_all(jnp.broadcast_to(hidden[None], (planes,) + hidden.shape), ("y", "side"), 0, 0, tiled=True)
    summed, kept = run_experts(rows, gain, share, (w_gate, w_up, w_down), other, hgs)
    quarter = width // hgs
    lanes = kept.shape[2] // 2
    own_piece, oth_piece = kept[..., :cols], kept[..., lanes:lanes + cols]
    kept = jnp.where(core == 0, jnp.concatenate([own_piece, oth_piece]), jnp.concatenate([oth_piece, own_piece]))
    kept = kept.transpose(1, 0, 2).reshape(toks, quarter)
    parts = lax.all_to_all(summed, ("hg", "y", "side"), 0, 0, tiled=True)
    moe = jnp.sum(parts.astype(F32), axis=0)
    moe = jnp.concatenate([moe[:toks], moe[toks:]], axis=1)
    return (kept.astype(F32) + moe).astype(BF)


def solution(mesh):
    devices = mesh.devices
    fine = Mesh(devices.reshape(4, 4, 2, 4), ("hg", "y", "c", "side"))
    grp = ("y", "c")
    plane = ("y", "c", "side")
    in_specs = (
        P(plane, "hg"),
        P(plane, "hg"),
        P("hg", None, None),
        P(plane, None, None),
        P(plane, None, None),
        P(plane),
        P("hg", None, None),
        P("hg", plane),
        P(plane, None),
        P(),
        P(plane, None),
        P(plane, None),
        P(grp, None, ("hg", "side")),
        P(grp, None, ("hg", "side")),
        P(grp, ("hg", "side"), None),
    )
    return jax.shard_map(body, mesh=fine, in_specs=in_specs, out_specs=P(plane, "hg"), check_vma=False)
```

```python
import functools

import jax
import jax.numpy as jnp
from jax import lax
from jax.experimental import pallas as pl
from jax.experimental.pallas import tpu as pltpu
from jax.sharding import Mesh
from jax.sharding import PartitionSpec as P

LAT = 512
ROPE = 64
NOPE = 128
VDIM = 128
QPR = 2
LEN = 4096
EPS = 1e-06
ROUTE_SCALE = 2.5
BF = jnp.bfloat16
F32 = jnp.float32

PAIRS_A = [(0, 1), (1, 0), (2, 3), (3, 2)]
PAIRS_B = [(1, 2), (2, 1), (3, 0), (0, 3)]
SWAP = [(0, 1), (1, 0)]


def attention_kernel(len_hbm, routes_hbm, ints_hbm, qn_hbm, qr_hbm, res_hbm, wa_hbm, lat_hbm, rope_hbm, wv_hbm, out_ref,
                     len_ref, routes_ref, ints_ref, qn_ref, qr_ref, res_ref, sem_in, wa, wv, lat, rope, qs, qps, os, ext, sc, sem_w, sem_l, sem_r, *, span, ahead, sides, experts):
    reqs, length, width = lat_hbm.shape
    heads = wa_hbm.shape[0]
    toks = qn_hbm.shape[0]
    qpr = toks // reqs
    rows = qpr * heads
    spans = length // span
    lanes = width // 128
    scale = (NOPE + ROPE) ** (-0.5)
    absorb = pltpu.make_async_copy(wa_hbm, wa, sem_w.at[0])
    small = [
        pltpu.make_async_copy(a, b, sem_in.at[k])
        for k, (a, b) in enumerate((
            (len_hbm, len_ref), (routes_hbm, routes_ref), (ints_hbm, ints_ref),
            (qn_hbm, qn_ref), (qr_hbm, qr_ref), (res_hbm, res_ref),
        ))
    ]
    for copy in small:
        copy.start()
    absorb.start()
    value = pltpu.make_async_copy(wv_hbm, wv, sem_w.at[1])

    def copies(r, i):
        at = pl.ds(i * span, span)
        return (
            pltpu.make_async_copy(lat_hbm.at[r, at, :], lat.at[r, at, :], sem_l.at[r * spans + i]),
            pltpu.make_async_copy(rope_hbm.at[r, :, at], rope.at[r, :, at], sem_r.at[r * spans + i]),
        )

    chunks = [(r, i) for r in range(reqs) for i in range(spans)]

    def begin(k):
        if k == len(chunks):
            value.start(priority=1)
        elif k < len(chunks):
            r, i = chunks[k]

            def go():
                for copy in copies(r, i):
                    copy.start(priority=1)

            if i == 0:
                go()
            else:
                pl.when(i * span < len_ref[r])(go)

    begin(0)
    for copy in small:
        copy.wait()
    for k in range(1, ahead):
        begin(k)
    planes = out_ref.shape[0]
    cores = 2
    n_val = heads * VDIM
    cols = res_ref.shape[1] // (planes * cores)
    which = lax.broadcasted_iota(jnp.int32, res_ref.shape, 0) == lax.axis_index("hg")
    row = jnp.sum(jnp.where(which, res_ref[...].astype(F32), 0.0), axis=0, keepdims=True)
    lane = lax.broadcasted_iota(jnp.int32, (1, 128), 1)
    dense = jnp.zeros((1, 128), jnp.int32)
    for j in range(toks):
        for k in range(routes_ref.shape[1]):
            dense = dense + jnp.where(lane == j * experts + routes_ref[j, k], ints_ref[j, k], 0)
    dense = dense.astype(F32)
    for p in range(planes):
        y, side = divmod(p, sides)
        for c in range(cores):
            start = ((y * cores + c) * sides + side) * cols // 128
            for t in range(3):
                tile = min(start + t, res_ref.shape[1] // 128 - 1)
                ext[p, pl.ds(t, 1), c * 128:(c + 1) * 128] = row[:, tile * 128:(tile + 1) * 128]
        ext[p, pl.ds(3, 1), :] = jnp.concatenate([dense, dense], axis=1)
    for p in range(planes):
        out_ref[p, :, n_val:] = ext[p].astype(BF)
    turned = qr_ref[...].astype(F32)
    for h in range(heads):
        pair = turned[:, (h // 2) * 2 * ROPE:(h // 2 + 1) * 2 * ROPE]
        if h % 2:
            pair = jnp.concatenate([pair[:, ROPE:], pair[:, :ROPE]], axis=1)
        qps[pl.ds(h, toks, stride=heads), :] = pair
    absorb.wait()
    for h in range(heads):
        latent = jnp.dot(qn_ref[:, h * NOPE:(h + 1) * NOPE], wa[h], preferred_element_type=F32)
        for c in range(lanes):
            qs[c, pl.ds(h, toks, stride=heads), :] = latent[:, c * 128:(c + 1) * 128]
    def scores(r, count):
        at = pl.ds(r * rows, rows)
        query = jnp.concatenate([qs[c, at, :] for c in range(lanes)], axis=1).astype(BF)
        rotary = qps[at, :ROPE].astype(BF)
        limit = len_ref[r] - qpr + lax.broadcasted_iota(jnp.int32, (rows, 1), 0) // heads
        out = []
        for i in range(count):
            to = pl.ds(i * span, span)
            for copy in copies(r, i):
                copy.wait()
            s = lax.dot_general(query, lat[r, to, :], (((1,), (1,)), ((), ())), preferred_element_type=F32)
            s = (s + jnp.dot(rotary, rope[r, :, to], preferred_element_type=F32)) * scale
            position = i * span + lax.broadcasted_iota(jnp.int32, (rows, span), 1)
            out.append(jnp.where(position <= limit, s, -jnp.inf))
        return out

    def mix(r, s):
        top = functools.reduce(jnp.maximum, [jnp.max(x, axis=1, keepdims=True) for x in s])
        p = [jnp.exp(x - top) for x in s]
        norm = sum(jnp.sum(x, axis=1, keepdims=True) for x in p)
        acc = sum(
            jnp.dot(x.astype(BF), lat[r, pl.ds(i * span, span), :], preferred_element_type=F32)
            for i, x in enumerate(p)
        )
        result = acc / norm
        for c in range(lanes):
            os[c, pl.ds(r * rows, rows), :] = result[:, c * 128:(c + 1) * 128]

    def attend(first, second):
        one = scores(0, first)
        two = scores(1, second)
        mix(0, one)
        mix(1, two)

    counts = [(len_ref[r] + span - 1) // span for r in range(reqs)]
    for first in range(1, spans + 1):
        for second in range(1, spans + 1):
            pl.when((counts[0] == first) & (counts[1] == second))(functools.partial(attend, first, second))
    value.wait()
    for h in range(heads):
        at = pl.ds(h, toks, stride=heads)
        o = jnp.concatenate([os[c, at, :] for c in range(lanes)], axis=1).astype(BF)
        head = jnp.dot(o, wv[h], preferred_element_type=F32).astype(BF)
        for k in range(planes):
            out_ref[k, :, h * VDIM:(h + 1) * VDIM] = head


def attention(q_nope, q_rope, w_absorb, cache_latent, cache_rope, lengths, w_value, residual, routes, gate_int,
              planes, sides, experts, span=2048, ahead=5):
    reqs, length, width = cache_latent.shape
    spans = length // span
    heads = w_absorb.shape[0]
    toks = q_nope.shape[0]
    hbm = pl.BlockSpec(memory_space=pltpu.HBM)
    vmem = pl.BlockSpec(memory_space=pltpu.VMEM)
    return pl.pallas_call(
        functools.partial(attention_kernel, span=span, ahead=ahead, sides=sides, experts=experts),
        out_shape=pltpu.VMEM((planes, toks, heads * VDIM + 256), BF),
        in_specs=[hbm] * 10,
        out_specs=vmem,
        scratch_shapes=[
            pltpu.SMEM(lengths.shape, jnp.int32),
            pltpu.SMEM(routes.shape, jnp.int32),
            pltpu.SMEM(gate_int.shape, jnp.int32),
            pltpu.VMEM(q_nope.shape, BF),
            pltpu.VMEM(q_rope.shape, BF),
            pltpu.VMEM(residual.shape, BF),
            pltpu.SemaphoreType.DMA((6,)),
            pltpu.VMEM(w_absorb.shape, BF),
            pltpu.VMEM(w_value.shape, BF),
            pltpu.VMEM(cache_latent.shape, BF),
            pltpu.VMEM(cache_rope.shape, BF),
            pltpu.VMEM((width // 128, toks * heads, 128), F32),
            pltpu.VMEM((toks * heads, 2 * ROPE), F32),
            pltpu.VMEM((width // 128, toks * heads, 128), F32),
            pltpu.VMEM((planes, toks, 256), F32),
            pltpu.VMEM((reqs, toks * heads // reqs, length), F32),
            pltpu.SemaphoreType.DMA((2,)),
            pltpu.SemaphoreType.DMA((reqs * spans,)),
            pltpu.SemaphoreType.DMA((reqs * spans,)),
        ],
        compiler_params=pltpu.CompilerParams(vmem_limit_bytes=20 * 1024 * 1024),
        name="attention",
    )(*(
        pltpu.with_memory_space_constraint(a, pltpu.HBM)
        for a in (lengths, routes, gate_int, q_nope, q_rope, residual, w_absorb, cache_latent, cache_rope, w_value)
    ))


def experts_kernel(rows_ref, gain_ref, share_ref, wg0, wu0, wd0, wg1, wu1, wd1, out_ref, kept_ref,
                   wg, wu, wd, sem, sem_down, *, ahead):
    local, depth, units = wg0.shape
    experts = 2 * local
    blocks = rows_ref.shape[0]
    stripes, sides, span = gain_ref.shape
    cols = span // 2
    rows = blocks * kept_ref.shape[1]
    stripe = depth // stripes
    core = lax.axis_index("c")
    groups = []
    for y in range(stripes):
        at = pl.ds(y * stripe, stripe)
        groups.append([
            pltpu.make_async_copy(src.at[:, at, :], dst.at[pl.ds(k * local, local), at, :], sem.at[y * 4 + 2 * k + j])
            for k in range(2)
            for j, (src, dst) in enumerate((((wg0, wg1)[k], wg), ((wu0, wu1)[k], wu)))
        ])
    messages, lines, tile = out_ref.shape
    toks = lines // 2
    parts = depth // (2 * tile)
    downs = []
    for n in range(parts):
        at = pl.ds(2 * n * tile, 2 * tile)
        downs.append([
            pltpu.make_async_copy(src.at[:, :, at], wd.at[pl.ds(k * local, local), :, at], sem_down.at[n * 2 + k])
            for k, src in enumerate((wd0, wd1))
        ])
    queue = groups + downs
    for y in range(ahead):
        for copy in groups[y]:
            copy.start()
    pick_rows(rows_ref, kept_ref)
    acc = [jnp.zeros((rows, 2 * units), F32) for _ in range(experts)]
    square = jnp.zeros((rows, span), F32)
    for y in range(stripes):
        for copy in queue[y + ahead]:
            copy.start()
        for copy in groups[y]:
            copy.wait()
        for s in range(sides):
            block = unpack(rows_ref[y * sides + s])
            square = square + block * block
            scaled = (block * gain_ref[y, pl.ds(s, 1), :]).astype(BF)
            own, oth = (
                pl.ds(pl.multiple_of(y * stripe + part * (stripe // 2) + s * cols, 16), cols)
                for part in (core, 1 - core)
            )
            for e in range(experts):
                both = jnp.concatenate(
                    [jnp.concatenate([wg[e, at, :], wu[e, at, :]], axis=1) for at in (own, oth)], axis=0
                )
                acc[e] = acc[e] + jnp.dot(scaled, both, preferred_element_type=F32)
    inverse = lax.rsqrt(jnp.sum(square, axis=-1, keepdims=True) / depth + EPS)
    acts = []
    for e in range(experts):
        both = acc[e] * inverse
        gate, up = both[:, :units], both[:, units:]
        share = share_ref[:, e:e + 1]
        act = gate / (1.0 + jnp.exp(-gate)) * up
        acts.append(jnp.where(share > 0, act * share, 0.0).astype(BF))
    act = jnp.concatenate(acts, axis=1)
    for n in range(parts):
        if stripes + n + ahead < len(queue):
            for copy in queue[stripes + n + ahead]:
                copy.start()
        for copy in downs[n]:
            copy.wait()
        down = wd[:, :, 2 * n * tile:(2 * n + 2) * tile].reshape(experts * units, 2 * tile)
        left = jnp.dot(act, down[:, :tile], preferred_element_type=F32)
        right = jnp.dot(act, down[:, tile:], preferred_element_type=F32)
        for k in range(blocks):
            at = slice(k * toks, (k + 1) * toks)
            out_ref[n * blocks + k] = jnp.concatenate([left[at], right[at]], axis=0).astype(BF)


def unpack(block):
    block = block.astype(F32)
    rows = block.shape[0] * 2 // 7
    last = block[3 * rows:]
    last = jnp.concatenate([last, pltpu.roll(last, 64, 1)], axis=0)
    return jnp.concatenate([block[:rows], block[rows:2 * rows], block[2 * rows:3 * rows], last[:, :64]], axis=1)


def pick_rows(blocks_ref, kept_ref):
    sides, toks, _ = kept_ref.shape
    at = (lax.axis_index("y") * sides + lax.axis_index("side")) * toks
    for s in range(sides):
        rows = unpack(blocks_ref[lax.axis_index("hg") * sides + s])
        found = rows[:toks]
        for k in range(1, rows.shape[0] // toks):
            found = jnp.where(at == k * toks, rows[k * toks:(k + 1) * toks], found)
        kept_ref[s] = found.astype(BF)


def run_experts(rows, gain, share, own, other, hgs, ahead=3):
    local, depth, units = own[0].shape
    experts = 2 * local
    blocks = rows.shape[0]
    stripes, sides, span = gain.shape
    toks = rows.shape[1] * rows.shape[2] // span // blocks
    count = blocks * toks
    vmem = pl.BlockSpec(memory_space=pltpu.VMEM)
    hbm = pl.BlockSpec(memory_space=pltpu.HBM)
    weights = [pltpu.with_memory_space_constraint(a, pltpu.HBM) for a in (*own, *other)]
    return pl.pallas_call(
        functools.partial(experts_kernel, ahead=ahead),
        out_shape=(
            pltpu.VMEM((hgs * blocks, 2 * toks, depth // hgs // 2), BF),
            jax.ShapeDtypeStruct((sides, toks, span), BF),
        ),
        in_specs=[vmem] * 3 + [hbm] * 6,
        out_specs=[vmem] * 2,
        scratch_shapes=[
            pltpu.VMEM((experts, depth, units), BF),
            pltpu.VMEM((experts, depth, units), BF),
            pltpu.VMEM((experts, units, depth), BF),
            pltpu.SemaphoreType.DMA((stripes * 4,)),
            pltpu.SemaphoreType.DMA((hgs * 2,)),
        ],
        compiler_params=pltpu.CompilerParams(vmem_limit_bytes=32 * 1024 * 1024),
        cost_estimate=pl.CostEstimate(flops=count * depth * 3072, bytes_accessed=24_000_000, transcendentals=0),
        name="experts",
    )(rows, gain, share, *weights)


def project_kernel(here_ref, own_ref, oth_ref, out_ref, xs, ext, *, n_val):
    planes, toks, _ = here_ref.shape
    cols = own_ref.shape[0]
    rows = planes * toks
    core = lax.axis_index("c")
    for p in range(planes):
        xs[pl.ds(p * toks, toks), :] = here_ref[p, :, :n_val].astype(F32)
        for c in range(2):
            tiles = here_ref[p, :, n_val + c * 128:n_val + (c + 1) * 128].astype(F32)
            for t in range(3):
                ext[c, pl.ds(p, 1), t * 128:(t + 1) * 128] = tiles[t:t + 1]
    x = xs[...].astype(BF)
    row = lax.broadcasted_iota(jnp.int32, (rows, planes), 0)
    col = lax.broadcasted_iota(jnp.int32, (rows, planes), 1)
    place = (row == col * toks + lax.axis_index("hg")).astype(BF)
    parts = []
    for w_ref, part in ((own_ref, core), (oth_ref, 1 - core)):
        block = (lax.axis_index("y") * 2 + part) * 4 + lax.axis_index("side")
        shift = lax.rem(block * cols, 128)
        window = jnp.where(part == 0, ext[0], ext[1])
        window = pltpu.roll(window, lax.rem(384 - shift, 384), 1)[:, :cols].astype(BF)
        product = lax.dot_general(x, w_ref[...], (((1,), (1,)), ((), ())), preferred_element_type=F32)
        parts.append(product + jnp.dot(place, window, preferred_element_type=F32))
    whole = jnp.concatenate(parts, axis=1)
    for t in range(3):
        out_ref[pl.ds(t * rows, rows), :] = whole[:, t * 128:(t + 1) * 128].astype(BF)
    last = jnp.concatenate([whole[:rows // 2, 384:], whole[rows // 2:, 384:]], axis=1)
    out_ref[pl.ds(3 * rows, rows // 2), :] = last.astype(BF)


def project(here, w_out, out_there, n_val):
    planes, toks, _ = here.shape
    vmem = pl.BlockSpec(memory_space=pltpu.VMEM)
    rows = planes * toks
    return pl.pallas_call(
        functools.partial(project_kernel, n_val=n_val),
        out_shape=pltpu.VMEM((rows * 7 // 2, 128), BF),
        in_specs=[vmem] * 3,
        out_specs=vmem,
        scratch_shapes=[pltpu.VMEM((rows, n_val), F32), pltpu.VMEM((2, planes, 384), F32)],
        compiler_params=pltpu.CompilerParams(vmem_limit_bytes=12 * 1024 * 1024),
        cost_estimate=pl.CostEstimate(flops=4 * rows * n_val * 224, bytes_accessed=2_500_000, transcendentals=0),
        name="project",
    )(here, w_out.T, out_there.T)


def body(
    q_nope, q_rope, w_absorb, cache_latent, cache_rope, lengths, w_value, w_out, residual, norm_gain,
    routes, gate_int, w_gate, w_up, w_down,
):
    hgs, ys, cores, sides = (lax.axis_size(a) for a in ("hg", "y", "c", "side"))
    hg, y, core, side = (lax.axis_index(a) for a in ("hg", "y", "c", "side"))
    planes = ys * sides
    toks, width = residual.shape
    cols = w_out.shape[1]
    local_experts = w_gate.shape[0]
    experts_all = local_experts * ys * cores

    message = attention(q_nope, q_rope, w_absorb, cache_latent, cache_rope, lengths, w_value, residual, routes, gate_int,
                        planes, sides, experts_all)
    message, w_out_, w_gate_, w_up_, w_down_ = lax.optimization_barrier((message, w_out, w_gate, w_up, w_down))
    out_there = lax.ppermute(w_out_, "c", SWAP)
    other = tuple(lax.ppermute(w, "c", SWAP) for w in (w_gate_, w_up_, w_down_))
    here = lax.all_to_all(message, ("y", "side"), 0, 0, tiled=True)
    n_val = w_absorb.shape[0] * VDIM
    partial = project(here, w_out, out_there, n_val)
    extra = here[..., n_val:]
    gates = extra[:, 3, :toks * experts_all].reshape(planes * toks, experts_all).astype(F32)
    total = jnp.sum(gates, axis=1, keepdims=True)
    share = jnp.concatenate(
        [
            lax.dynamic_slice_in_dim(gates, (y * cores + part) * local_experts, local_experts, 1)
            for part in (core, 1 - core)
        ],
        axis=1,
    ) * (ROUTE_SCALE / total)
    gain = norm_gain.astype(F32).reshape(ys, cores, sides, cols)
    gain = jnp.where(core == 0, gain, gain[:, ::-1]).transpose(0, 2, 1, 3).reshape(ys, sides, cores * cols)
    got, share, gain = lax.optimization_barrier((lax.ppermute(partial, "hg", PAIRS_A), share, gain))
    pair = (partial.astype(F32) + got.astype(F32)).astype(BF)
    hidden = (pair.astype(F32) + lax.ppermute(pair, "hg", PAIRS_B).astype(F32)).astype(BF)

    rows = lax.all_to_all(jnp.broadcast_to(hidden[None], (planes,) + hidden.shape), ("y", "side"), 0, 0, tiled=True)
    summed, kept = run_experts(rows, gain, share, (w_gate, w_up, w_down), other, hgs)
    quarter = width // hgs
    own_piece, oth_piece = kept[..., :cols], kept[..., cols:]
    kept = jnp.where(core == 0, jnp.concatenate([own_piece, oth_piece]), jnp.concatenate([oth_piece, own_piece]))
    kept = kept.transpose(1, 0, 2).reshape(toks, quarter)
    parts = lax.all_to_all(summed, ("hg", "y", "side"), 0, 0, tiled=True)
    moe = jnp.sum(parts.astype(F32), axis=0)
    moe = jnp.concatenate([moe[:toks], moe[toks:]], axis=1)
    return (kept.astype(F32) + moe).astype(BF)


def solution(mesh):
    devices = mesh.devices
    fine = Mesh(devices.reshape(4, 4, 2, 4), ("hg", "y", "c", "side"))
    grp = ("y", "c")
    plane = ("y", "c", "side")
    in_specs = (
        P(plane, "hg"),
        P(plane, "hg"),
        P("hg", None, None),
        P(plane, None, None),
        P(plane, None, None),
        P(plane),
        P("hg", None, None),
        P("hg", plane),
        P(plane, None),
        P(),
        P(plane, None),
        P(plane, None),
        P(grp, None, ("hg", "side")),
        P(grp, None, ("hg", "side")),
        P(grp, ("hg", "side"), None),
    )
    return jax.shard_map(body, mesh=fine, in_specs=in_specs, out_specs=P(plane, "hg"), check_vma=False)
```

```python
import functools

import jax
import jax.numpy as jnp
from jax import lax
from jax.experimental import pallas as pl
from jax.experimental.pallas import tpu as pltpu
from jax.sharding import Mesh
from jax.sharding import PartitionSpec as P

LAT = 512
ROPE = 64
NOPE = 128
VDIM = 128
QPR = 2
LEN = 4096
EPS = 1e-06
ROUTE_SCALE = 2.5
BF = jnp.bfloat16
F32 = jnp.float32

PAIRS_A = [(0, 1), (1, 0), (2, 3), (3, 2)]
PAIRS_B = [(1, 2), (2, 1), (3, 0), (0, 3)]
SWAP = [(0, 1), (1, 0)]


def attention_kernel(len_hbm, routes_hbm, ints_hbm, qn_hbm, qr_hbm, res_hbm, wa_hbm, lat_hbm, rope_hbm, wv_hbm, out_ref,
                     len_ref, routes_ref, ints_ref, qn_ref, qr_ref, res_ref, sem_in, wa, wv, lat, rope, qs, qps, os, ext, sc, sem_w, sem_l, sem_r, *, span, ahead, sides, experts):
    reqs, length, width = lat_hbm.shape
    heads = wa_hbm.shape[0]
    toks = qn_hbm.shape[0]
    qpr = toks // reqs
    rows = qpr * heads
    spans = length // span
    lanes = width // 128
    scale = (NOPE + ROPE) ** (-0.5)
    absorb = pltpu.make_async_copy(wa_hbm, wa, sem_w.at[0])
    small = [
        pltpu.make_async_copy(a, b, sem_in.at[k])
        for k, (a, b) in enumerate((
            (len_hbm, len_ref), (routes_hbm, routes_ref), (ints_hbm, ints_ref),
            (qn_hbm, qn_ref), (qr_hbm, qr_ref), (res_hbm, res_ref),
        ))
    ]
    for copy in small:
        copy.start()
    absorb.start()
    value = pltpu.make_async_copy(wv_hbm, wv, sem_w.at[1])

    def copies(r, i):
        at = pl.ds(i * span, span)
        return (
            pltpu.make_async_copy(lat_hbm.at[r, at, :], lat.at[r, at, :], sem_l.at[r * spans + i]),
            pltpu.make_async_copy(rope_hbm.at[r, :, at], rope.at[r, :, at], sem_r.at[r * spans + i]),
        )

    chunks = [(r, i) for r in range(reqs) for i in range(spans)]

    def begin(k):
        if k == len(chunks):
            value.start(priority=1)
        elif k < len(chunks):
            r, i = chunks[k]

            def go():
                for copy in copies(r, i):
                    copy.start(priority=1)

            if i == 0:
                go()
            else:
                pl.when(i * span < len_ref[r])(go)

    begin(0)
    for copy in small:
        copy.wait()
    for k in range(1, ahead):
        begin(k)
    planes = out_ref.shape[0]
    cores = 2
    n_val = heads * VDIM
    cols = res_ref.shape[1] // (planes * cores)
    which = lax.broadcasted_iota(jnp.int32, res_ref.shape, 0) == lax.axis_index("hg")
    row = jnp.sum(jnp.where(which, res_ref[...].astype(F32), 0.0), axis=0, keepdims=True)
    lane = lax.broadcasted_iota(jnp.int32, (1, 128), 1)
    dense = jnp.zeros((1, 128), jnp.int32)
    for j in range(toks):
        for k in range(routes_ref.shape[1]):
            dense = dense + jnp.where(lane == j * experts + routes_ref[j, k], ints_ref[j, k], 0)
    dense = dense.astype(F32)
    for p in range(planes):
        y, side = divmod(p, sides)
        for c in range(cores):
            start = ((y * cores + c) * sides + side) * cols // 128
            for t in range(3):
                tile = min(start + t, res_ref.shape[1] // 128 - 1)
                ext[p, pl.ds(t, 1), c * 128:(c + 1) * 128] = row[:, tile * 128:(tile + 1) * 128]
        ext[p, pl.ds(3, 1), :] = jnp.concatenate([dense, dense], axis=1)
    for p in range(planes):
        out_ref[p, :, n_val:] = ext[p].astype(BF)
    turned = qr_ref[...].astype(F32)
    for h in range(heads):
        pair = turned[:, (h // 2) * 2 * ROPE:(h // 2 + 1) * 2 * ROPE]
        if h % 2:
            pair = jnp.concatenate([pair[:, ROPE:], pair[:, :ROPE]], axis=1)
        qps[pl.ds(h, toks, stride=heads), :] = pair
    absorb.wait()
    for h in range(heads):
        latent = jnp.dot(qn_ref[:, h * NOPE:(h + 1) * NOPE], wa[h], preferred_element_type=F32)
        for c in range(lanes):
            qs[c, pl.ds(h, toks, stride=heads), :] = latent[:, c * 128:(c + 1) * 128]
    def scores(r, count):
        at = pl.ds(r * rows, rows)
        query = jnp.concatenate([qs[c, at, :] for c in range(lanes)], axis=1).astype(BF)
        rotary = qps[at, :ROPE].astype(BF)
        limit = len_ref[r] - qpr + lax.broadcasted_iota(jnp.int32, (rows, 1), 0) // heads
        out = []
        for i in range(count):
            to = pl.ds(i * span, span)
            for copy in copies(r, i):
                copy.wait()
            s = lax.dot_general(query, lat[r, to, :], (((1,), (1,)), ((), ())), preferred_element_type=F32)
            s = (s + jnp.dot(rotary, rope[r, :, to], preferred_element_type=F32)) * scale
            position = i * span + lax.broadcasted_iota(jnp.int32, (rows, span), 1)
            out.append(jnp.where(position <= limit, s, -jnp.inf))
        return out

    def mix(r, s):
        top = functools.reduce(jnp.maximum, [jnp.max(x, axis=1, keepdims=True) for x in s])
        p = [jnp.exp(x - top) for x in s]
        norm = sum(jnp.sum(x, axis=1, keepdims=True) for x in p)
        acc = sum(
            jnp.dot(x.astype(BF), lat[r, pl.ds(i * span, span), :], preferred_element_type=F32)
            for i, x in enumerate(p)
        )
        result = acc / norm
        for c in range(lanes):
            os[c, pl.ds(r * rows, rows), :] = result[:, c * 128:(c + 1) * 128]

    def attend(first, second):
        one = scores(0, first)
        two = scores(1, second)
        mix(0, one)
        mix(1, two)

    counts = [(len_ref[r] + span - 1) // span for r in range(reqs)]
    for first in range(1, spans + 1):
        for second in range(1, spans + 1):
            pl.when((counts[0] == first) & (counts[1] == second))(functools.partial(attend, first, second))
    value.wait()
    for h in range(heads):
        at = pl.ds(h, toks, stride=heads)
        o = jnp.concatenate([os[c, at, :] for c in range(lanes)], axis=1).astype(BF)
        head = jnp.dot(o, wv[h], preferred_element_type=F32).astype(BF)
        for k in range(planes):
            out_ref[k, :, h * VDIM:(h + 1) * VDIM] = head


def attention(q_nope, q_rope, w_absorb, cache_latent, cache_rope, lengths, w_value, residual, routes, gate_int,
              planes, sides, experts, span=2048, ahead=5):
    reqs, length, width = cache_latent.shape
    spans = length // span
    heads = w_absorb.shape[0]
    toks = q_nope.shape[0]
    hbm = pl.BlockSpec(memory_space=pltpu.HBM)
    vmem = pl.BlockSpec(memory_space=pltpu.VMEM)
    return pl.pallas_call(
        functools.partial(attention_kernel, span=span, ahead=ahead, sides=sides, experts=experts),
        out_shape=pltpu.VMEM((planes, toks, heads * VDIM + 256), BF),
        in_specs=[hbm] * 10,
        out_specs=vmem,
        scratch_shapes=[
            pltpu.SMEM(lengths.shape, jnp.int32),
            pltpu.SMEM(routes.shape, jnp.int32),
            pltpu.SMEM(gate_int.shape, jnp.int32),
            pltpu.VMEM(q_nope.shape, BF),
            pltpu.VMEM(q_rope.shape, BF),
            pltpu.VMEM(residual.shape, BF),
            pltpu.SemaphoreType.DMA((6,)),
            pltpu.VMEM(w_absorb.shape, BF),
            pltpu.VMEM(w_value.shape, BF),
            pltpu.VMEM(cache_latent.shape, BF),
            pltpu.VMEM(cache_rope.shape, BF),
            pltpu.VMEM((width // 128, toks * heads, 128), F32),
            pltpu.VMEM((toks * heads, 2 * ROPE), F32),
            pltpu.VMEM((width // 128, toks * heads, 128), F32),
            pltpu.VMEM((planes, toks, 256), F32),
            pltpu.VMEM((reqs, toks * heads // reqs, length), F32),
            pltpu.SemaphoreType.DMA((2,)),
            pltpu.SemaphoreType.DMA((reqs * spans,)),
            pltpu.SemaphoreType.DMA((reqs * spans,)),
        ],
        compiler_params=pltpu.CompilerParams(vmem_limit_bytes=20 * 1024 * 1024),
        name="attention",
    )(*(
        pltpu.with_memory_space_constraint(a, pltpu.HBM)
        for a in (lengths, routes, gate_int, q_nope, q_rope, residual, w_absorb, cache_latent, cache_rope, w_value)
    ))


def fetch_kernel(w_ref, o_ref, sem):
    copy = pltpu.make_async_copy(w_ref.at[:, pl.ds(0, o_ref.shape[1]), :], o_ref, sem)
    copy.start()
    copy.wait()


def fetch(w, rows, name):
    return pl.pallas_call(
        fetch_kernel,
        out_shape=pltpu.VMEM((w.shape[0], rows, w.shape[2]), w.dtype),
        in_specs=[pl.BlockSpec(memory_space=pltpu.HBM)],
        out_specs=pl.BlockSpec(memory_space=pl.ANY),
        scratch_shapes=[pltpu.SemaphoreType.DMA],
        cost_estimate=pl.CostEstimate(flops=0, bytes_accessed=4_000_000, transcendentals=0),
        compiler_params=pltpu.CompilerParams(vmem_limit_bytes=4 * 1024 * 1024),
        name=name,
    )(pltpu.with_memory_space_constraint(w, pltpu.HBM))


def experts_kernel(rows_ref, gain_ref, share_ref, pre_g, pre_u, wg0, wu0, wd0, wg1, wu1, wd1, out_ref, kept_ref,
                   wg, wu, wd, sem, sem_down, *, ahead):
    local, depth, units = wg0.shape
    experts = 2 * local
    blocks = rows_ref.shape[0]
    stripes, sides, span = gain_ref.shape
    cols = span // 2
    rows = blocks * kept_ref.shape[1]
    stripe = depth // stripes
    core = lax.axis_index("c")
    groups = []
    for y in range(stripes):
        at = pl.ds(y * stripe, stripe)
        groups.append([
            pltpu.make_async_copy(
                pre.at[:, at, :] if k == 0 and (y + 1) * stripe <= pre.shape[1] else src.at[:, at, :], dst.at[pl.ds(k * local, local), at, :], sem.at[y * 4 + 2 * k + j]
            )
            for k in range(2)
            for j, (src, dst, pre) in enumerate((((wg0, wg1)[k], wg, pre_g), ((wu0, wu1)[k], wu, pre_u)))
        ])
    messages, lines, tile = out_ref.shape
    toks = lines // 2
    parts = depth // (2 * tile)
    downs = []
    for n in range(parts):
        at = pl.ds(2 * n * tile, 2 * tile)
        downs.append([
            pltpu.make_async_copy(src.at[:, :, at], wd.at[pl.ds(k * local, local), :, at], sem_down.at[n * 2 + k])
            for k, src in enumerate((wd0, wd1))
        ])
    queue = groups + downs
    for y in range(ahead):
        for copy in groups[y]:
            copy.start()
    pick_rows(rows_ref, kept_ref)
    acc = [jnp.zeros((rows, 2 * units), F32) for _ in range(experts)]
    square = jnp.zeros((rows, span), F32)
    for y in range(stripes):
        for copy in queue[y + ahead]:
            copy.start()
        for copy in groups[y]:
            copy.wait()
        for s in range(sides):
            block = unpack(rows_ref[y * sides + s])
            square = square + block * block
            scaled = (block * gain_ref[y, pl.ds(s, 1), :]).astype(BF)
            own, oth = (
                pl.ds(pl.multiple_of(y * stripe + part * (stripe // 2) + s * cols, 16), cols)
                for part in (core, 1 - core)
            )
            for e in range(experts):
                both = jnp.concatenate(
                    [jnp.concatenate([wg[e, at, :], wu[e, at, :]], axis=1) for at in (own, oth)], axis=0
                )
                acc[e] = acc[e] + jnp.dot(scaled, both, preferred_element_type=F32)
    inverse = lax.rsqrt(jnp.sum(square, axis=-1, keepdims=True) / depth + EPS)
    acts = []
    for e in range(experts):
        both = acc[e] * inverse
        gate, up = both[:, :units], both[:, units:]
        share = share_ref[:, e:e + 1]
        act = gate / (1.0 + jnp.exp(-gate)) * up
        acts.append(jnp.where(share > 0, act * share, 0.0).astype(BF))
    act = jnp.concatenate(acts, axis=1)
    for n in range(parts):
        if stripes + n + ahead < len(queue):
            for copy in queue[stripes + n + ahead]:
                copy.start()
        for copy in downs[n]:
            copy.wait()
        down = wd[:, :, 2 * n * tile:(2 * n + 2) * tile].reshape(experts * units, 2 * tile)
        left = jnp.dot(act, down[:, :tile], preferred_element_type=F32)
        right = jnp.dot(act, down[:, tile:], preferred_element_type=F32)
        for k in range(blocks):
            at = slice(k * toks, (k + 1) * toks)
            out_ref[n * blocks + k] = jnp.concatenate([left[at], right[at]], axis=0).astype(BF)


def unpack(block):
    block = block.astype(F32)
    rows = block.shape[0] * 2 // 7
    last = block[3 * rows:]
    last = jnp.concatenate([last, pltpu.roll(last, 64, 1)], axis=0)
    return jnp.concatenate([block[:rows], block[rows:2 * rows], block[2 * rows:3 * rows], last[:, :64]], axis=1)


def pick_rows(blocks_ref, kept_ref):
    sides, toks, _ = kept_ref.shape
    at = (lax.axis_index("y") * sides + lax.axis_index("side")) * toks
    for s in range(sides):
        rows = unpack(blocks_ref[lax.axis_index("hg") * sides + s])
        found = rows[:toks]
        for k in range(1, rows.shape[0] // toks):
            found = jnp.where(at == k * toks, rows[k * toks:(k + 1) * toks], found)
        kept_ref[s] = found.astype(BF)


def run_experts(rows, gain, share, early, own, other, hgs, ahead=3):
    local, depth, units = own[0].shape
    experts = 2 * local
    blocks = rows.shape[0]
    stripes, sides, span = gain.shape
    toks = rows.shape[1] * rows.shape[2] // span // blocks
    count = blocks * toks
    vmem = pl.BlockSpec(memory_space=pltpu.VMEM)
    hbm = pl.BlockSpec(memory_space=pltpu.HBM)
    weights = [pltpu.with_memory_space_constraint(a, pltpu.HBM) for a in (*own, *other)]
    return pl.pallas_call(
        functools.partial(experts_kernel, ahead=ahead),
        out_shape=(
            pltpu.VMEM((hgs * blocks, 2 * toks, depth // hgs // 2), BF),
            jax.ShapeDtypeStruct((sides, toks, span), BF),
        ),
        in_specs=[vmem] * 3 + [pl.BlockSpec(memory_space=pl.ANY)] * 2 + [hbm] * 6,
        out_specs=[vmem] * 2,
        scratch_shapes=[
            pltpu.VMEM((experts, depth, units), BF),
            pltpu.VMEM((experts, depth, units), BF),
            pltpu.VMEM((experts, units, depth), BF),
            pltpu.SemaphoreType.DMA((stripes * 4,)),
            pltpu.SemaphoreType.DMA((hgs * 2,)),
        ],
        compiler_params=pltpu.CompilerParams(vmem_limit_bytes=32 * 1024 * 1024),
        cost_estimate=pl.CostEstimate(flops=count * depth * 3072, bytes_accessed=24_000_000, transcendentals=0),
        name="experts",
    )(rows, gain, share, *early, *weights)


def project_kernel(here_ref, own_ref, oth_ref, out_ref, xs, ext, *, n_val):
    planes, toks, _ = here_ref.shape
    cols = own_ref.shape[0]
    rows = planes * toks
    core = lax.axis_index("c")
    for p in range(planes):
        xs[pl.ds(p * toks, toks), :] = here_ref[p, :, :n_val].astype(F32)
        for c in range(2):
            tiles = here_ref[p, :, n_val + c * 128:n_val + (c + 1) * 128].astype(F32)
            for t in range(3):
                ext[c, pl.ds(p, 1), t * 128:(t + 1) * 128] = tiles[t:t + 1]
    x = xs[...].astype(BF)
    row = lax.broadcasted_iota(jnp.int32, (rows, planes), 0)
    col = lax.broadcasted_iota(jnp.int32, (rows, planes), 1)
    place = (row == col * toks + lax.axis_index("hg")).astype(BF)
    parts = []
    for w_ref, part in ((own_ref, core), (oth_ref, 1 - core)):
        block = (lax.axis_index("y") * 2 + part) * 4 + lax.axis_index("side")
        shift = lax.rem(block * cols, 128)
        window = jnp.where(part == 0, ext[0], ext[1])
        window = pltpu.roll(window, lax.rem(384 - shift, 384), 1)[:, :cols].astype(BF)
        product = lax.dot_general(x, w_ref[...], (((1,), (1,)), ((), ())), preferred_element_type=F32)
        parts.append(product + jnp.dot(place, window, preferred_element_type=F32))
    whole = jnp.concatenate(parts, axis=1)
    for t in range(3):
        out_ref[pl.ds(t * rows, rows), :] = whole[:, t * 128:(t + 1) * 128].astype(BF)
    last = jnp.concatenate([whole[:rows // 2, 384:], whole[rows // 2:, 384:]], axis=1)
    out_ref[pl.ds(3 * rows, rows // 2), :] = last.astype(BF)


def project(here, w_out, out_there, n_val):
    planes, toks, _ = here.shape
    vmem = pl.BlockSpec(memory_space=pltpu.VMEM)
    rows = planes * toks
    return pl.pallas_call(
        functools.partial(project_kernel, n_val=n_val),
        out_shape=pltpu.VMEM((rows * 7 // 2, 128), BF),
        in_specs=[vmem] * 3,
        out_specs=vmem,
        scratch_shapes=[pltpu.VMEM((rows, n_val), F32), pltpu.VMEM((2, planes, 384), F32)],
        compiler_params=pltpu.CompilerParams(vmem_limit_bytes=12 * 1024 * 1024),
        cost_estimate=pl.CostEstimate(flops=4 * rows * n_val * 224, bytes_accessed=2_500_000, transcendentals=0),
        name="project",
    )(here, w_out.T, out_there.T)


def body(
    q_nope, q_rope, w_absorb, cache_latent, cache_rope, lengths, w_value, w_out, residual, norm_gain,
    routes, gate_int, w_gate, w_up, w_down,
):
    hgs, ys, cores, sides = (lax.axis_size(a) for a in ("hg", "y", "c", "side"))
    hg, y, core, side = (lax.axis_index(a) for a in ("hg", "y", "c", "side"))
    planes = ys * sides
    toks, width = residual.shape
    cols = w_out.shape[1]
    local_experts = w_gate.shape[0]
    experts_all = local_experts * ys * cores

    message = attention(q_nope, q_rope, w_absorb, cache_latent, cache_rope, lengths, w_value, residual, routes, gate_int,
                        planes, sides, experts_all)
    message, w_out_, w_gate_, w_up_, w_down_ = lax.optimization_barrier((message, w_out, w_gate, w_up, w_down))
    out_there = lax.ppermute(w_out_, "c", SWAP)
    other = tuple(lax.ppermute(w, "c", SWAP) for w in (w_gate_, w_up_, w_down_))
    here = lax.all_to_all(message, ("y", "side"), 0, 0, tiled=True)
    n_val = w_absorb.shape[0] * VDIM
    partial = project(here, w_out, out_there, n_val)
    extra = here[..., n_val:]
    gates = extra[:, 3, :toks * experts_all].reshape(planes * toks, experts_all).astype(F32)
    total = jnp.sum(gates, axis=1, keepdims=True)
    share = jnp.concatenate(
        [
            lax.dynamic_slice_in_dim(gates, (y * cores + part) * local_experts, local_experts, 1)
            for part in (core, 1 - core)
        ],
        axis=1,
    ) * (ROUTE_SCALE / total)
    gain = norm_gain.astype(F32).reshape(ys, cores, sides, cols)
    gain = jnp.where(core == 0, gain, gain[:, ::-1]).transpose(0, 2, 1, 3).reshape(ys, sides, cores * cols)
    partial, w_gate_ = lax.optimization_barrier((partial, w_gate))
    gate_early = fetch(w_gate_, w_gate.shape[1], "fetch_gate")
    got, share, gain, gate_early = lax.optimization_barrier((lax.ppermute(partial, "hg", PAIRS_A), share, gain, gate_early))
    pair = (partial.astype(F32) + got.astype(F32)).astype(BF)
    pair, w_up_ = lax.optimization_barrier((pair, w_up))
    up_early = fetch(w_up_, w_up.shape[1], "fetch_up")
    got, up_early = lax.optimization_barrier((lax.ppermute(pair, "hg", PAIRS_B), up_early))
    hidden = (pair.astype(F32) + got.astype(F32)).astype(BF)

    rows = lax.all_to_all(jnp.broadcast_to(hidden[None], (planes,) + hidden.shape), ("y", "side"), 0, 0, tiled=True)
    summed, kept = run_experts(rows, gain, share, (gate_early, up_early), (w_gate, w_up, w_down), other, hgs)
    quarter = width // hgs
    own_piece, oth_piece = kept[..., :cols], kept[..., cols:]
    kept = jnp.where(core == 0, jnp.concatenate([own_piece, oth_piece]), jnp.concatenate([oth_piece, own_piece]))
    kept = kept.transpose(1, 0, 2).reshape(toks, quarter)
    parts = lax.all_to_all(summed, ("hg", "y", "side"), 0, 0, tiled=True)
    moe = jnp.sum(parts.astype(F32), axis=0)
    moe = jnp.concatenate([moe[:toks], moe[toks:]], axis=1)
    return (kept.astype(F32) + moe).astype(BF)


def solution(mesh):
    devices = mesh.devices
    fine = Mesh(devices.reshape(4, 4, 2, 4), ("hg", "y", "c", "side"))
    grp = ("y", "c")
    plane = ("y", "c", "side")
    in_specs = (
        P(plane, "hg"),
        P(plane, "hg"),
        P("hg", None, None),
        P(plane, None, None),
        P(plane, None, None),
        P(plane),
        P("hg", None, None),
        P("hg", plane),
        P(plane, None),
        P(),
        P(plane, None),
        P(plane, None),
        P(grp, None, ("hg", "side")),
        P(grp, None, ("hg", "side")),
        P(grp, ("hg", "side"), None),
    )
    return jax.shard_map(body, mesh=fine, in_specs=in_specs, out_specs=P(plane, "hg"), check_vma=False)
```

```python
import functools

import jax
import jax.numpy as jnp
from jax import lax
from jax.experimental import pallas as pl
from jax.experimental.pallas import tpu as pltpu
from jax.sharding import Mesh
from jax.sharding import PartitionSpec as P

LAT = 512
ROPE = 64
NOPE = 128
VDIM = 128
QPR = 2
LEN = 4096
EPS = 1e-06
ROUTE_SCALE = 2.5
BF = jnp.bfloat16
F32 = jnp.float32

PAIRS_A = [(0, 1), (1, 0), (2, 3), (3, 2)]
PAIRS_B = [(1, 2), (2, 1), (3, 0), (0, 3)]
SWAP = [(0, 1), (1, 0)]


def attention_kernel(len_hbm, routes_hbm, ints_hbm, qn_hbm, qr_hbm, res_hbm, wa_hbm, lat_hbm, rope_hbm, wv_hbm, out_ref,
                     len_ref, routes_ref, ints_ref, qn_ref, qr_ref, res_ref, sem_in, wa, wv, lat, rope, qs, qps, os, ext, sc, sem_w, sem_l, sem_r, *, span, ahead, sides, experts):
    reqs, length, width = lat_hbm.shape
    heads = wa_hbm.shape[0]
    toks = qn_hbm.shape[0]
    qpr = toks // reqs
    rows = qpr * heads
    spans = length // span
    lanes = width // 128
    scale = (NOPE + ROPE) ** (-0.5)
    absorb = pltpu.make_async_copy(wa_hbm, wa, sem_w.at[0])
    small = [
        pltpu.make_async_copy(a, b, sem_in.at[k])
        for k, (a, b) in enumerate((
            (len_hbm, len_ref), (routes_hbm, routes_ref), (ints_hbm, ints_ref),
            (qn_hbm, qn_ref), (qr_hbm, qr_ref), (res_hbm, res_ref),
        ))
    ]
    for copy in small:
        copy.start()
    absorb.start()
    value = pltpu.make_async_copy(wv_hbm, wv, sem_w.at[1])

    def copies(r, i):
        at = pl.ds(i * span, span)
        return (
            pltpu.make_async_copy(lat_hbm.at[r, at, :], lat.at[r, at, :], sem_l.at[r * spans + i]),
            pltpu.make_async_copy(rope_hbm.at[r, :, at], rope.at[r, :, at], sem_r.at[r * spans + i]),
        )

    chunks = [(r, i) for r in range(reqs) for i in range(spans)]

    def begin(k):
        if k == len(chunks):
            value.start(priority=1)
        elif k < len(chunks):
            r, i = chunks[k]

            def go():
                for copy in copies(r, i):
                    copy.start(priority=1)

            if i == 0:
                go()
            else:
                pl.when(i * span < len_ref[r])(go)

    begin(0)
    for copy in small:
        copy.wait()
    for k in range(1, ahead):
        begin(k)
    planes = out_ref.shape[0]
    cores = 2
    n_val = heads * VDIM
    cols = res_ref.shape[1] // (planes * cores)
    which = lax.broadcasted_iota(jnp.int32, res_ref.shape, 0) == lax.axis_index("hg")
    row = jnp.sum(jnp.where(which, res_ref[...].astype(F32), 0.0), axis=0, keepdims=True)
    lane = lax.broadcasted_iota(jnp.int32, (1, 128), 1)
    dense = jnp.zeros((1, 128), jnp.int32)
    for j in range(toks):
        for k in range(routes_ref.shape[1]):
            dense = dense + jnp.where(lane == j * experts + routes_ref[j, k], ints_ref[j, k], 0)
    dense = dense.astype(F32)
    for p in range(planes):
        y, side = divmod(p, sides)
        for c in range(cores):
            start = ((y * cores + c) * sides + side) * cols // 128
            for t in range(3):
                tile = min(start + t, res_ref.shape[1] // 128 - 1)
                ext[p, pl.ds(t, 1), c * 128:(c + 1) * 128] = row[:, tile * 128:(tile + 1) * 128]
        ext[p, pl.ds(3, 1), :] = jnp.concatenate([dense, dense], axis=1)
    for p in range(planes):
        out_ref[p, :, n_val:] = ext[p].astype(BF)
    turned = qr_ref[...].astype(F32)
    for h in range(heads):
        pair = turned[:, (h // 2) * 2 * ROPE:(h // 2 + 1) * 2 * ROPE]
        if h % 2:
            pair = jnp.concatenate([pair[:, ROPE:], pair[:, :ROPE]], axis=1)
        qps[pl.ds(h, toks, stride=heads), :] = pair
    absorb.wait()
    for h in range(heads):
        latent = jnp.dot(qn_ref[:, h * NOPE:(h + 1) * NOPE], wa[h], preferred_element_type=F32)
        for c in range(lanes):
            qs[c, pl.ds(h, toks, stride=heads), :] = latent[:, c * 128:(c + 1) * 128]
    def scores(r, count):
        at = pl.ds(r * rows, rows)
        query = jnp.concatenate([qs[c, at, :] for c in range(lanes)], axis=1).astype(BF)
        rotary = qps[at, :ROPE].astype(BF)
        limit = len_ref[r] - qpr + lax.broadcasted_iota(jnp.int32, (rows, 1), 0) // heads
        out = []
        for i in range(count):
            to = pl.ds(i * span, span)
            for copy in copies(r, i):
                copy.wait()
            s = lax.dot_general(query, lat[r, to, :], (((1,), (1,)), ((), ())), preferred_element_type=F32)
            s = (s + jnp.dot(rotary, rope[r, :, to], preferred_element_type=F32)) * scale
            position = i * span + lax.broadcasted_iota(jnp.int32, (rows, span), 1)
            out.append(jnp.where(position <= limit, s, -jnp.inf))
        return out

    def mix(r, s):
        top = functools.reduce(jnp.maximum, [jnp.max(x, axis=1, keepdims=True) for x in s])
        p = [jnp.exp(x - top) for x in s]
        norm = sum(jnp.sum(x, axis=1, keepdims=True) for x in p)
        acc = sum(
            jnp.dot(x.astype(BF), lat[r, pl.ds(i * span, span), :], preferred_element_type=F32)
            for i, x in enumerate(p)
        )
        result = acc / norm
        for c in range(lanes):
            os[c, pl.ds(r * rows, rows), :] = result[:, c * 128:(c + 1) * 128]

    def attend(first, second):
        one = scores(0, first)
        two = scores(1, second)
        mix(0, one)
        mix(1, two)

    counts = [(len_ref[r] + span - 1) // span for r in range(reqs)]
    for first in range(1, spans + 1):
        for second in range(1, spans + 1):
            pl.when((counts[0] == first) & (counts[1] == second))(functools.partial(attend, first, second))
    value.wait()
    for h in range(heads):
        at = pl.ds(h, toks, stride=heads)
        o = jnp.concatenate([os[c, at, :] for c in range(lanes)], axis=1).astype(BF)
        head = jnp.dot(o, wv[h], preferred_element_type=F32).astype(BF)
        for k in range(planes):
            out_ref[k, :, h * VDIM:(h + 1) * VDIM] = head


def attention(q_nope, q_rope, w_absorb, cache_latent, cache_rope, lengths, w_value, residual, routes, gate_int,
              planes, sides, experts, span=2048, ahead=5):
    reqs, length, width = cache_latent.shape
    spans = length // span
    heads = w_absorb.shape[0]
    toks = q_nope.shape[0]
    hbm = pl.BlockSpec(memory_space=pltpu.HBM)
    vmem = pl.BlockSpec(memory_space=pltpu.VMEM)
    return pl.pallas_call(
        functools.partial(attention_kernel, span=span, ahead=ahead, sides=sides, experts=experts),
        out_shape=pltpu.VMEM((planes, toks, heads * VDIM + 256), BF),
        in_specs=[hbm] * 10,
        out_specs=vmem,
        scratch_shapes=[
            pltpu.SMEM(lengths.shape, jnp.int32),
            pltpu.SMEM(routes.shape, jnp.int32),
            pltpu.SMEM(gate_int.shape, jnp.int32),
            pltpu.VMEM(q_nope.shape, BF),
            pltpu.VMEM(q_rope.shape, BF),
            pltpu.VMEM(residual.shape, BF),
            pltpu.SemaphoreType.DMA((6,)),
            pltpu.VMEM(w_absorb.shape, BF),
            pltpu.VMEM(w_value.shape, BF),
            pltpu.VMEM(cache_latent.shape, BF),
            pltpu.VMEM(cache_rope.shape, BF),
            pltpu.VMEM((width // 128, toks * heads, 128), F32),
            pltpu.VMEM((toks * heads, 2 * ROPE), F32),
            pltpu.VMEM((width // 128, toks * heads, 128), F32),
            pltpu.VMEM((planes, toks, 256), F32),
            pltpu.VMEM((reqs, toks * heads // reqs, length), F32),
            pltpu.SemaphoreType.DMA((2,)),
            pltpu.SemaphoreType.DMA((reqs * spans,)),
            pltpu.SemaphoreType.DMA((reqs * spans,)),
        ],
        compiler_params=pltpu.CompilerParams(vmem_limit_bytes=20 * 1024 * 1024),
        name="attention",
    )(*(
        pltpu.with_memory_space_constraint(a, pltpu.HBM)
        for a in (lengths, routes, gate_int, q_nope, q_rope, residual, w_absorb, cache_latent, cache_rope, w_value)
    ))


def fetch_kernel(*refs):
    count = len(refs) // 2
    copies = [pltpu.make_async_copy(refs[k], refs[count + k], refs[-1].at[k]) for k in range(count)]
    for copy in copies:
        copy.start()
    for copy in copies:
        copy.wait()


def fetch(arrays, name):
    return pl.pallas_call(
        fetch_kernel,
        out_shape=tuple(pltpu.VMEM(w.shape, w.dtype) for w in arrays),
        in_specs=[pl.BlockSpec(memory_space=pltpu.HBM)] * len(arrays),
        out_specs=[pl.BlockSpec(memory_space=pl.ANY)] * len(arrays),
        scratch_shapes=[pltpu.SemaphoreType.DMA((len(arrays),))],
        cost_estimate=pl.CostEstimate(flops=0, bytes_accessed=4_000_000, transcendentals=0),
        compiler_params=pltpu.CompilerParams(vmem_limit_bytes=4 * 1024 * 1024),
        name=name,
    )(*(pltpu.with_memory_space_constraint(w, pltpu.HBM) for w in arrays))


def experts_kernel(rows_ref, gain_ref, share_ref, pre_g, pre_u, pre_d, wg0, wu0, wd0, wg1, wu1, wd1, out_ref, kept_ref,
                   wg, wu, wd, sem, sem_down, *, ahead):
    local, depth, units = wg0.shape
    experts = 2 * local
    blocks = rows_ref.shape[0]
    stripes, sides, span = gain_ref.shape
    cols = span // 2
    rows = blocks * kept_ref.shape[1]
    stripe = depth // stripes
    core = lax.axis_index("c")
    groups = []
    for y in range(stripes):
        at = pl.ds(y * stripe, stripe)
        groups.append([
            pltpu.make_async_copy(
                pre.at[:, at, :] if k == 0 and (y + 1) * stripe <= pre.shape[1] else src.at[:, at, :], dst.at[pl.ds(k * local, local), at, :], sem.at[y * 4 + 2 * k + j]
            )
            for k in range(2)
            for j, (src, dst, pre) in enumerate((((wg0, wg1)[k], wg, pre_g), ((wu0, wu1)[k], wu, pre_u)))
        ])
    messages, lines, tile = out_ref.shape
    toks = lines // 2
    parts = depth // (2 * tile)
    downs = []
    for n in range(parts):
        at = pl.ds(2 * n * tile, 2 * tile)
        downs.append([
            pltpu.make_async_copy(src.at[:, :, at], wd.at[pl.ds(k * local, local), :, at], sem_down.at[n * 2 + k])
            for k, src in enumerate((pre_d, wd1))
        ])
    queue = groups + downs
    for y in range(ahead):
        for copy in groups[y]:
            copy.start()
    pick_rows(rows_ref, kept_ref)
    acc = [jnp.zeros((rows, 2 * units), F32) for _ in range(experts)]
    square = jnp.zeros((rows, span), F32)
    for y in range(stripes):
        for copy in queue[y + ahead]:
            copy.start()
        for copy in groups[y]:
            copy.wait()
        for s in range(sides):
            block = unpack(rows_ref[y * sides + s])
            square = square + block * block
            scaled = (block * gain_ref[y, pl.ds(s, 1), :]).astype(BF)
            own, oth = (
                pl.ds(pl.multiple_of(y * stripe + part * (stripe // 2) + s * cols, 16), cols)
                for part in (core, 1 - core)
            )
            for e in range(experts):
                both = jnp.concatenate(
                    [jnp.concatenate([wg[e, at, :], wu[e, at, :]], axis=1) for at in (own, oth)], axis=0
                )
                acc[e] = acc[e] + jnp.dot(scaled, both, preferred_element_type=F32)
    inverse = lax.rsqrt(jnp.sum(square, axis=-1, keepdims=True) / depth + EPS)
    acts = []
    for e in range(experts):
        both = acc[e] * inverse
        gate, up = both[:, :units], both[:, units:]
        share = share_ref[:, e:e + 1]
        act = gate / (1.0 + jnp.exp(-gate)) * up
        acts.append(jnp.where(share > 0, act * share, 0.0).astype(BF))
    act = jnp.concatenate(acts, axis=1)
    for n in range(parts):
        if stripes + n + ahead < len(queue):
            for copy in queue[stripes + n + ahead]:
                copy.start()
        for copy in downs[n]:
            copy.wait()
        down = wd[:, :, 2 * n * tile:(2 * n + 2) * tile].reshape(experts * units, 2 * tile)
        left = jnp.dot(act, down[:, :tile], preferred_element_type=F32)
        right = jnp.dot(act, down[:, tile:], preferred_element_type=F32)
        for k in range(blocks):
            at = slice(k * toks, (k + 1) * toks)
            out_ref[n * blocks + k] = jnp.concatenate([left[at], right[at]], axis=0).astype(BF)


def unpack(block):
    block = block.astype(F32)
    rows = block.shape[0] * 2 // 7
    last = block[3 * rows:]
    last = jnp.concatenate([last, pltpu.roll(last, 64, 1)], axis=0)
    return jnp.concatenate([block[:rows], block[rows:2 * rows], block[2 * rows:3 * rows], last[:, :64]], axis=1)


def pick_rows(blocks_ref, kept_ref):
    sides, toks, _ = kept_ref.shape
    at = (lax.axis_index("y") * sides + lax.axis_index("side")) * toks
    for s in range(sides):
        rows = unpack(blocks_ref[lax.axis_index("hg") * sides + s])
        found = rows[:toks]
        for k in range(1, rows.shape[0] // toks):
            found = jnp.where(at == k * toks, rows[k * toks:(k + 1) * toks], found)
        kept_ref[s] = found.astype(BF)


def run_experts(rows, gain, share, early, own, other, hgs, ahead=3):
    local, depth, units = own[0].shape
    experts = 2 * local
    blocks = rows.shape[0]
    stripes, sides, span = gain.shape
    toks = rows.shape[1] * rows.shape[2] // span // blocks
    count = blocks * toks
    vmem = pl.BlockSpec(memory_space=pltpu.VMEM)
    hbm = pl.BlockSpec(memory_space=pltpu.HBM)
    weights = [pltpu.with_memory_space_constraint(a, pltpu.HBM) for a in (*own, *other)]
    return pl.pallas_call(
        functools.partial(experts_kernel, ahead=ahead),
        out_shape=(
            pltpu.VMEM((hgs * blocks, 2 * toks, depth // hgs // 2), BF),
            jax.ShapeDtypeStruct((sides, toks, span), BF),
        ),
        in_specs=[vmem] * 3 + [pl.BlockSpec(memory_space=pl.ANY)] * 3 + [hbm] * 6,
        out_specs=[vmem] * 2,
        scratch_shapes=[
            pltpu.VMEM((experts, depth, units), BF),
            pltpu.VMEM((experts, depth, units), BF),
            pltpu.VMEM((experts, units, depth), BF),
            pltpu.SemaphoreType.DMA((stripes * 4,)),
            pltpu.SemaphoreType.DMA((hgs * 2,)),
        ],
        compiler_params=pltpu.CompilerParams(vmem_limit_bytes=32 * 1024 * 1024),
        cost_estimate=pl.CostEstimate(flops=count * depth * 3072, bytes_accessed=24_000_000, transcendentals=0),
        name="experts",
    )(rows, gain, share, *early, *weights)


def project_kernel(here_ref, own_ref, oth_ref, out_ref, xs, ext, *, n_val):
    planes, toks, _ = here_ref.shape
    cols = own_ref.shape[0]
    rows = planes * toks
    core = lax.axis_index("c")
    for p in range(planes):
        xs[pl.ds(p * toks, toks), :] = here_ref[p, :, :n_val].astype(F32)
        for c in range(2):
            tiles = here_ref[p, :, n_val + c * 128:n_val + (c + 1) * 128].astype(F32)
            for t in range(3):
                ext[c, pl.ds(p, 1), t * 128:(t + 1) * 128] = tiles[t:t + 1]
    x = xs[...].astype(BF)
    row = lax.broadcasted_iota(jnp.int32, (rows, planes), 0)
    col = lax.broadcasted_iota(jnp.int32, (rows, planes), 1)
    place = (row == col * toks + lax.axis_index("hg")).astype(BF)
    parts = []
    for w_ref, part in ((own_ref, core), (oth_ref, 1 - core)):
        block = (lax.axis_index("y") * 2 + part) * 4 + lax.axis_index("side")
        shift = lax.rem(block * cols, 128)
        window = jnp.where(part == 0, ext[0], ext[1])
        window = pltpu.roll(window, lax.rem(384 - shift, 384), 1)[:, :cols].astype(BF)
        product = lax.dot_general(x, w_ref[...], (((1,), (1,)), ((), ())), preferred_element_type=F32)
        parts.append(product + jnp.dot(place, window, preferred_element_type=F32))
    whole = jnp.concatenate(parts, axis=1)
    for t in range(3):
        out_ref[pl.ds(t * rows, rows), :] = whole[:, t * 128:(t + 1) * 128].astype(BF)
    last = jnp.concatenate([whole[:rows // 2, 384:], whole[rows // 2:, 384:]], axis=1)
    out_ref[pl.ds(3 * rows, rows // 2), :] = last.astype(BF)


def project(here, w_out, out_there, n_val):
    planes, toks, _ = here.shape
    vmem = pl.BlockSpec(memory_space=pltpu.VMEM)
    rows = planes * toks
    return pl.pallas_call(
        functools.partial(project_kernel, n_val=n_val),
        out_shape=pltpu.VMEM((rows * 7 // 2, 128), BF),
        in_specs=[vmem] * 3,
        out_specs=vmem,
        scratch_shapes=[pltpu.VMEM((rows, n_val), F32), pltpu.VMEM((2, planes, 384), F32)],
        compiler_params=pltpu.CompilerParams(vmem_limit_bytes=12 * 1024 * 1024),
        cost_estimate=pl.CostEstimate(flops=4 * rows * n_val * 224, bytes_accessed=2_500_000, transcendentals=0),
        name="project",
    )(here, w_out.T, out_there.T)


def body(
    q_nope, q_rope, w_absorb, cache_latent, cache_rope, lengths, w_value, w_out, residual, norm_gain,
    routes, gate_int, w_gate, w_up, w_down,
):
    hgs, ys, cores, sides = (lax.axis_size(a) for a in ("hg", "y", "c", "side"))
    hg, y, core, side = (lax.axis_index(a) for a in ("hg", "y", "c", "side"))
    planes = ys * sides
    toks, width = residual.shape
    cols = w_out.shape[1]
    local_experts = w_gate.shape[0]
    experts_all = local_experts * ys * cores

    message = attention(q_nope, q_rope, w_absorb, cache_latent, cache_rope, lengths, w_value, residual, routes, gate_int,
                        planes, sides, experts_all)
    message, w_out_, w_gate_, w_up_, w_down_ = lax.optimization_barrier((message, w_out, w_gate, w_up, w_down))
    out_there = lax.ppermute(w_out_, "c", SWAP)
    other = tuple(lax.ppermute(w, "c", SWAP) for w in (w_gate_, w_up_, w_down_))
    here = lax.all_to_all(message, ("y", "side"), 0, 0, tiled=True)
    n_val = w_absorb.shape[0] * VDIM
    partial = project(here, w_out, out_there, n_val)
    extra = here[..., n_val:]
    gates = extra[:, 3, :toks * experts_all].reshape(planes * toks, experts_all).astype(F32)
    total = jnp.sum(gates, axis=1, keepdims=True)
    share = jnp.concatenate(
        [
            lax.dynamic_slice_in_dim(gates, (y * cores + part) * local_experts, local_experts, 1)
            for part in (core, 1 - core)
        ],
        axis=1,
    ) * (ROUTE_SCALE / total)
    gain = norm_gain.astype(F32).reshape(ys, cores, sides, cols)
    gain = jnp.where(core == 0, gain, gain[:, ::-1]).transpose(0, 2, 1, 3).reshape(ys, sides, cores * cols)
    partial, w_gate_ = lax.optimization_barrier((partial, w_gate))
    (gate_early,) = fetch((w_gate_,), "fetch_gate")
    got, share, gain, gate_early = lax.optimization_barrier((lax.ppermute(partial, "hg", PAIRS_A), share, gain, gate_early))
    pair = (partial.astype(F32) + got.astype(F32)).astype(BF)
    pair, w_up_, w_down_ = lax.optimization_barrier((pair, w_up, w_down))
    up_early, down_early = fetch((w_up_, w_down_), "fetch_up_down")
    got, up_early, down_early = lax.optimization_barrier((lax.ppermute(pair, "hg", PAIRS_B), up_early, down_early))
    hidden = (pair.astype(F32) + got.astype(F32)).astype(BF)

    rows = lax.all_to_all(jnp.broadcast_to(hidden[None], (planes,) + hidden.shape), ("y", "side"), 0, 0, tiled=True)
    summed, kept = run_experts(rows, gain, share, (gate_early, up_early, down_early), (w_gate, w_up, w_down), other, hgs)
    quarter = width // hgs
    own_piece, oth_piece = kept[..., :cols], kept[..., cols:]
    kept = jnp.where(core == 0, jnp.concatenate([own_piece, oth_piece]), jnp.concatenate([oth_piece, own_piece]))
    kept = kept.transpose(1, 0, 2).reshape(toks, quarter)
    parts = lax.all_to_all(summed, ("hg", "y", "side"), 0, 0, tiled=True)
    moe = jnp.sum(parts.astype(F32), axis=0)
    moe = jnp.concatenate([moe[:toks], moe[toks:]], axis=1)
    return (kept.astype(F32) + moe).astype(BF)


def solution(mesh):
    devices = mesh.devices
    fine = Mesh(devices.reshape(4, 4, 2, 4), ("hg", "y", "c", "side"))
    grp = ("y", "c")
    plane = ("y", "c", "side")
    in_specs = (
        P(plane, "hg"),
        P(plane, "hg"),
        P("hg", None, None),
        P(plane, None, None),
        P(plane, None, None),
        P(plane),
        P("hg", None, None),
        P("hg", plane),
        P(plane, None),
        P(),
        P(plane, None),
        P(plane, None),
        P(grp, None, ("hg", "side")),
        P(grp, None, ("hg", "side")),
        P(grp, ("hg", "side"), None),
    )
    return jax.shard_map(body, mesh=fine, in_specs=in_specs, out_specs=P(plane, "hg"), check_vma=False)
```
